32 devices in a mesh: segment: 2 (over x), dp: 4 (over z), mp: 4 (over y, core).
Axes of the slice: x: 2, y: 2, z: 4, core: 2. Of those that a mesh axis runs over, the one named last changes fastest.
Arguments:
- patch_tokens: bfloat16 [32, 16, 3072], P('dp', None, 'mp'), may hold values from -400 to 400
- visible_index: int32 [32, 16], P('dp'), may hold values from 0 to 63, as said below
- output_grad: bfloat16 [32, 16, 3072], P('dp', None, 'mp'), may hold values from -1.5 to 1.5
- norm_gain: float32 [2, 3072], P('segment'), may hold values from 0.1 to 1.9
- master_weights: float32 [2, 12288, 2048], P('segment', 'dp', 'mp'), may hold values from -2 to 2
- first_moment: float32 [2, 12288, 2048], P('segment', 'dp', 'mp'), may hold values from -6 to 6
- second_moment: float32 [2, 12288, 2048], P('segment', 'dp', 'mp'), may hold values from 0.01 to 1
Outputs:
- new_master: float32 [2, 12288, 2048], P('segment', 'dp', 'mp')
- new_first: float32 [2, 12288, 2048], P('segment', 'dp', 'mp')
- new_second: float32 [2, 12288, 2048], P('segment', 'dp', 'mp')
The draws below stay inside these ranges and needn't reach their ends.
Inputs may be any that keep to these rules, and one draw needn't show every extreme that they name: `visible_index`: in each volume the 16 indices are distinct and increasing.
All inputs are finite; a program needn't handle non-finite values.
Results may differ from the reference program's by a relative error of at most 0.02.
Values may be sent and summed in bfloat16 or wider, within the bound.
A program may use at most 192 MiB of HBM per device.

```python
import math
import jax
import jax.numpy as jnp
from jax import lax

D = 3072
HEADS = 16
HD = 128
PATCHES = 64
VIS = 16
VOLS = 32
SEGMENTS = 2
HEAD_GROUPS = 4


def draw_visible_index(key, part):
    subkeys = jax.random.split(key, VOLS)

    def pick_patches(subkey):
        return jax.random.permutation(subkey, PATCHES)[:VIS]
    chosen = jax.vmap(pick_patches)(subkeys)
    return jnp.sort(chosen, axis=1).astype(jnp.int32)


def draw_patch_tokens(key, part):
    base_key = jax.random.fold_in(key, 0)
    values = jax.random.truncated_normal(base_key, -6.0, 6.0, (VOLS, VIS, D), jnp.float32)
    return values.astype(jnp.bfloat16)


def draw_master_weights(key, part):
    base_key = jax.random.fold_in(key, 0)
    col_count = HEADS * HD
    row_std = jnp.where(jnp.arange(4 * D) < 3 * D, D ** (-0.5), col_count ** (-0.5)).astype(jnp.float32)[None, :, None]
    return jax.random.truncated_normal(base_key, -6.0, 6.0, (SEGMENTS, 4 * D, col_count), jnp.float32) * row_std


def steps_of(rng, shape, shards, smallest, top_value):
    level, own = 1.0, jax.random.fold_in(rng, 6)
    for axis_at, blocks in shards:
        steps = jnp.exp(jax.random.uniform(jax.random.fold_in(own, axis_at), (blocks,), jnp.float32, smallest / len(shards), top_value / len(shards)))
        level = level * jnp.repeat(steps, shape[axis_at] // blocks).reshape([-1 if axis == axis_at else 1 for axis in range(len(shape))])
    return level


def scatter_about(key, shape, spread, limit, cuts=(), kind=jnp.bfloat16):
    array = jax.random.normal(key, shape, jnp.float32) * spread
    if len(cuts) > 0:
        array = steps_of(key, shape, cuts, -0.22, 0.18) * array
    return jnp.clip(array, min=-limit, max=limit).astype(kind)


def setup_inputs(seed: int = 0) -> dict:
    arg_keys = jax.random.split(jax.random.key(seed), 8)
    return {
        "patch_tokens": draw_patch_tokens(jax.random.fold_in(arg_keys[7], 71), 0),
        "visible_index": draw_visible_index(jax.random.fold_in(arg_keys[7], 71), 0),
        "output_grad": scatter_about(arg_keys[2], (VOLS, VIS, D), 0.25, 1.5, ((0, 4), (2, 4))),
        "norm_gain": jnp.clip(1.0 + 0.18 * jax.random.normal(arg_keys[3], (SEGMENTS, D), jnp.float32), 0.1, 1.9),
        "master_weights": draw_master_weights(jax.random.fold_in(arg_keys[7], 71), 0),
        "first_moment": scatter_about(arg_keys[5], (SEGMENTS, 4 * D, HEADS * HD), 1.0, 6.0, ((0, 2), (1, 4), (2, 4)), jnp.float32),
        "second_moment": jnp.clip(jnp.exp(math.log(1.0) - 4.6051702 * jax.random.uniform(arg_keys[6], (SEGMENTS, 4 * D, HEADS * HD), jnp.float32) ** steps_of(arg_keys[6], (SEGMENTS, 4 * D, HEADS * HD), ((0, 2), (1, 4), (2, 4)), -0.2, 0.2)), 0.01, 1.0),
    }


beta_one = 0.9
beta_two = 0.95
learn_rate = 0.01
decay_rate = 0.1
adam_eps = 1e-08
norm_eps = 1e-05
step_count = 10

def position_table(visible_index, model_width):
    half_width = model_width // 2
    angle_rate = jnp.exp(jnp.arange(half_width, dtype=jnp.float32) * (-2.0 * math.log(10000.0) / model_width))
    angles = visible_index.astype(jnp.float32)[..., None] * angle_rate
    return jnp.concatenate([jnp.sin(angles), jnp.cos(angles)], axis=-1)

def norm_forward(hidden, norm_scale):
    values = hidden.astype(jnp.float32)
    centred = values - lax.optimization_barrier(jnp.mean(values, axis=-1, keepdims=True))
    inverse_dev = lax.rsqrt(lax.optimization_barrier(jnp.mean(centred * centred, axis=-1, keepdims=True)) + norm_eps)
    standard = centred * inverse_dev
    return ((standard * norm_scale).astype(jnp.bfloat16), standard, inverse_dev)

def norm_backward(d_normed, d_output, standard, inverse_dev, norm_scale):
    scaled = d_normed * norm_scale
    inner = scaled - lax.optimization_barrier(jnp.mean(scaled, axis=-1, keepdims=True)) - standard * lax.optimization_barrier(jnp.mean(scaled * standard, axis=-1, keepdims=True))
    return (d_output.astype(jnp.float32) + inner * inverse_dev).astype(jnp.bfloat16)

def softmax_rows(scores):
    lifted = jnp.exp(scores - lax.optimization_barrier(jnp.max(scores, axis=-1, keepdims=True)))
    return lifted / lax.optimization_barrier(jnp.sum(lifted, axis=-1, keepdims=True))

def rounded(values):
    return lax.optimization_barrier(values.astype(jnp.bfloat16)).astype(jnp.float32)

def adam_update(gradient, master, first_moment, second_moment):
    new_first = beta_one * first_moment + (1.0 - beta_one) * gradient
    new_second = beta_two * second_moment + (1.0 - beta_two) * gradient * gradient
    direction = new_first / (1.0 - beta_one ** step_count) / (jnp.sqrt(new_second / (1.0 - beta_two ** step_count)) + adam_eps)
    new_master = master - learn_rate * (direction + decay_rate * master)
    return (new_master, new_first, new_second)

def reference(patch_tokens, visible_index, output_grad, norm_gain, master_weights, first_moment, second_moment):
    vol_count, length, model_width = patch_tokens.shape
    col_count = master_weights.shape[2]
    head_count = col_count // HD
    row_count = vol_count * length
    group_cols = col_count // HEAD_GROUPS
    score_scale = 1.0 / math.sqrt(HD)
    weights = master_weights.astype(jnp.bfloat16)
    first_input = (patch_tokens.astype(jnp.float32) + position_table(visible_index, model_width)).astype(jnp.bfloat16).reshape(row_count, model_width)

    def heads_view(values):
        return values.reshape(vol_count, length, head_count, HD).astype(jnp.float32)

    def forward(layer_in, segment_idx):
        layer_w = weights[segment_idx]
        normed, standard, inverse_dev = norm_forward(layer_in, norm_gain[segment_idx])
        queries = jnp.dot(normed, layer_w[:model_width], preferred_element_type=jnp.float32).astype(jnp.bfloat16)
        key_rows = jnp.dot(normed, layer_w[model_width:2 * model_width], preferred_element_type=jnp.float32).astype(jnp.bfloat16)
        values = jnp.dot(normed, layer_w[2 * model_width:3 * model_width], preferred_element_type=jnp.float32).astype(jnp.bfloat16)
        scores = jnp.einsum('vqhe,vkhe->vhqk', heads_view(queries), heads_view(key_rows)) * score_scale
        softmaxed = softmax_rows(scores)
        probs_half = softmaxed.astype(jnp.bfloat16)
        attended = jnp.einsum('vhqk,vkhe->vqhe', probs_half.astype(jnp.float32), heads_view(values))
        attended = attended.astype(jnp.bfloat16).reshape(row_count, col_count)
        return (normed, standard, inverse_dev, queries, key_rows, values, softmaxed, probs_half, attended)

    def mix(layer_in, attended, segment_idx):
        out_wt = weights[segment_idx, 3 * model_width:]
        total = jnp.zeros((row_count, model_width), jnp.float32)
        for group_idx in range(HEAD_GROUPS):
            lower = group_idx * group_cols
            piece = jnp.dot(attended[:, lower:lower + group_cols], out_wt[:, lower:lower + group_cols].T, preferred_element_type=jnp.float32)
            total = total + rounded(piece)
        return (layer_in.astype(jnp.float32) + total).astype(jnp.bfloat16)

    def backward(d_output, cache, segment_idx):
        normed, standard, inverse_dev, queries, key_rows, values, softmaxed, probs_half, attended = cache
        layer_w = weights[segment_idx]
        d_attended = jnp.dot(d_output, layer_w[3 * model_width:], preferred_element_type=jnp.float32).astype(jnp.bfloat16)
        d_heads = heads_view(d_attended)
        d_probs = jnp.einsum('vqhe,vkhe->vhqk', d_heads, heads_view(values))
        d_scores = (softmaxed * (d_probs - lax.optimization_barrier(jnp.sum(d_probs * softmaxed, axis=-1, keepdims=True))) * score_scale).astype(jnp.bfloat16)
        d_queries = jnp.einsum('vhqk,vkhe->vqhe', d_scores.astype(jnp.float32), heads_view(key_rows)).astype(jnp.bfloat16).reshape(row_count, col_count)
        d_keys = jnp.einsum('vhqk,vqhe->vkhe', d_scores.astype(jnp.float32), heads_view(queries)).astype(jnp.bfloat16).reshape(row_count, col_count)
        d_values = jnp.einsum('vhqk,vqhe->vkhe', probs_half.astype(jnp.float32), d_heads).astype(jnp.bfloat16).reshape(row_count, col_count)
        gradient = jnp.concatenate([jnp.dot(normed.T, d_queries, preferred_element_type=jnp.float32), jnp.dot(normed.T, d_keys, preferred_element_type=jnp.float32), jnp.dot(normed.T, d_values, preferred_element_type=jnp.float32), jnp.dot(d_output.T, attended, preferred_element_type=jnp.float32)], axis=0)
        return (d_queries, d_keys, d_values, gradient)

    def input_grad(d_output, cache, d_queries, d_keys, d_values, segment_idx):
        standard, inverse_dev = (cache[1], cache[2])
        layer_w = weights[segment_idx]
        d_normed = jnp.zeros((row_count, model_width), jnp.float32)
        for group_idx in range(HEAD_GROUPS):
            lower = group_idx * group_cols
            upper = lower + group_cols
            left = jnp.concatenate([d_queries[:, lower:upper], d_keys[:, lower:upper], d_values[:, lower:upper]], axis=1)
            right = jnp.concatenate([layer_w[:model_width, lower:upper], layer_w[model_width:2 * model_width, lower:upper], layer_w[2 * model_width:3 * model_width, lower:upper]], axis=1)
            d_normed = d_normed + rounded(jnp.dot(left, right.T, preferred_element_type=jnp.float32))
        return norm_backward(d_normed, d_output, standard, inverse_dev, norm_gain[segment_idx])
    cache_first = forward(first_input, 0)
    hidden_one = mix(first_input, cache_first[8], 0)
    cache_second = forward(hidden_one, 1)
    d_output_two = output_grad.reshape(row_count, model_width)
    d_queries, d_keys, d_values, grads_second = backward(d_output_two, cache_second, 1)
    d_hidden_one = input_grad(d_output_two, cache_second, d_queries, d_keys, d_values, 1)
    grads_first = backward(d_hidden_one, cache_first, 0)[3]
    gradient = jnp.stack([grads_first, grads_second])
    return adam_update(gradient, master_weights, first_moment, second_moment)
```

```python
import math

import jax
import jax.numpy as jnp
from jax import lax
from jax.sharding import PartitionSpec as P

HD = 128
MB_VOLS = 2


beta_one = 0.9
beta_two = 0.95
learn_rate = 0.01
decay_rate = 0.1
adam_eps = 1e-08
norm_eps = 1e-05
step_count = 10


def from_behind(array, axis, by):
    peers = lax.axis_size(axis)
    pairs = [(i, i + by) for i in range(peers) if 0 <= i + by < peers]
    return lax.ppermute(array, axis, pairs)


def position_table(visible_index, model_width):
    half_width = model_width // 2
    angle_rate = jnp.exp(
        jnp.arange(half_width, dtype=jnp.float32) * (-2.0 * math.log(10000.0) / model_width)
    )
    angles = visible_index.astype(jnp.float32)[..., None] * angle_rate
    return jnp.concatenate([jnp.sin(angles), jnp.cos(angles)], axis=-1)


def norm_forward(hidden, norm_scale):
    values = hidden.astype(jnp.float32)
    centred = values - jnp.mean(values, axis=-1, keepdims=True)
    inverse_dev = lax.rsqrt(jnp.mean(centred * centred, axis=-1, keepdims=True) + norm_eps)
    standard = centred * inverse_dev
    return ((standard * norm_scale).astype(jnp.bfloat16), standard, inverse_dev)


def norm_backward(d_normed, d_output, standard, inverse_dev, norm_scale):
    scaled = d_normed * norm_scale
    inner = (
        scaled
        - jnp.mean(scaled, axis=-1, keepdims=True)
        - standard * jnp.mean(scaled * standard, axis=-1, keepdims=True)
    )
    return (d_output.astype(jnp.float32) + inner * inverse_dev).astype(jnp.bfloat16)


def softmax_rows(scores):
    lifted = jnp.exp(scores - jnp.max(scores, axis=-1, keepdims=True))
    return lifted / jnp.sum(lifted, axis=-1, keepdims=True)


def rounded(values):
    return lax.optimization_barrier(values.astype(jnp.bfloat16)).astype(jnp.float32)


def adam_update(gradient, master, first_moment, second_moment):
    new_first = beta_one * first_moment + (1.0 - beta_one) * gradient
    new_second = beta_two * second_moment + (1.0 - beta_two) * gradient * gradient
    direction = (
        new_first
        / (1.0 - beta_one**step_count)
        / (jnp.sqrt(new_second / (1.0 - beta_two**step_count)) + adam_eps)
    )
    new_master = master - learn_rate * (direction + decay_rate * master)
    return (new_master, new_first, new_second)


def layer_local(layer_in, norm_scale, weights):
    row_count, model_width = layer_in.shape
    col_count = weights.shape[1]
    head_count = col_count // HD
    length = row_count // MB_VOLS
    normed, standard, inverse_dev = norm_forward(layer_in, norm_scale)
    triple = weights[: 3 * model_width].reshape(3, model_width, col_count)
    project = jnp.einsum("nd,sdc->nsc", normed, triple, preferred_element_type=jnp.float32).astype(
        jnp.bfloat16
    )
    shaped = project.reshape(MB_VOLS, length, 3, head_count, HD)
    scores = jnp.einsum(
        "vqhe,vkhe->vhqk", shaped[:, :, 0], shaped[:, :, 1], preferred_element_type=jnp.float32
    ) * (1.0 / math.sqrt(HD))
    softmaxed = softmax_rows(scores)
    probs_half = softmaxed.astype(jnp.bfloat16)
    attended = jnp.einsum(
        "vhqk,vkhe->vqhe", probs_half, shaped[:, :, 2], preferred_element_type=jnp.float32
    )
    attended = attended.astype(jnp.bfloat16).reshape(row_count, col_count)
    return (normed, standard, inverse_dev, project, softmaxed, probs_half, attended)


def head_terms(attended, weights, model_width):
    return rounded(
        jnp.einsum(
            "nc,dc->nd", attended, weights[3 * model_width :], preferred_element_type=jnp.float32
        )
    )


def attention_back(d_output, saved_vals, weights):
    project, softmaxed, probs_half = (saved_vals[3], saved_vals[4], saved_vals[5])
    row_count, model_width = d_output.shape
    col_count = weights.shape[1]
    head_count = col_count // HD
    length = row_count // MB_VOLS
    shaped = project.reshape(MB_VOLS, length, 3, head_count, HD)
    d_attended = jnp.einsum(
        "nd,dc->nc", d_output, weights[3 * model_width :], preferred_element_type=jnp.float32
    )
    d_attended = d_attended.astype(jnp.bfloat16).reshape(MB_VOLS, length, head_count, HD)
    d_probs = jnp.einsum(
        "vqhe,vkhe->vhqk", d_attended, shaped[:, :, 2], preferred_element_type=jnp.float32
    )
    d_scores = (
        softmaxed
        * (d_probs - jnp.sum(d_probs * softmaxed, axis=-1, keepdims=True))
        * (1.0 / math.sqrt(HD))
    ).astype(jnp.bfloat16)
    d_queries = jnp.einsum(
        "vhqk,vkhe->vqhe", d_scores, shaped[:, :, 1], preferred_element_type=jnp.float32
    ).astype(jnp.bfloat16)
    d_keys = jnp.einsum(
        "vhqk,vqhe->vkhe", d_scores, shaped[:, :, 0], preferred_element_type=jnp.float32
    ).astype(jnp.bfloat16)
    d_values = jnp.einsum(
        "vhqk,vqhe->vkhe", probs_half, d_attended, preferred_element_type=jnp.float32
    ).astype(jnp.bfloat16)
    return jnp.stack([d_queries, d_keys, d_values], axis=2).reshape(row_count, 3, col_count)


def feature_terms(d_project, weights, model_width):
    col_count = weights.shape[1]
    triple = weights[: 3 * model_width].reshape(3, model_width, col_count)
    return rounded(jnp.einsum("nsc,sdc->nd", d_project, triple, preferred_element_type=jnp.float32))


def shards(
    patch_tokens, visible_index, output_grad, norm_gain, master_weights, first_moment, second_moment
):
    model_width = patch_tokens.shape[2] * lax.axis_size("mp")
    rows_here = master_weights.shape[1]
    is_first = lax.axis_index("segment") == 0
    norm_scale = norm_gain[0]
    weights = lax.all_gather(master_weights[0].astype(jnp.bfloat16), "dp", axis=0, tiled=True)
    tokens_full, grads_full = (
        lax.all_gather(patch_tokens, "mp", axis=2, tiled=True),
        lax.all_gather(output_grad, "mp", axis=2, tiled=True),
    )
    vol_count, length = visible_index.shape
    micro_count = vol_count // MB_VOLS
    mb_rows = MB_VOLS * length
    first_inputs = (
        tokens_full.astype(jnp.float32) + position_table(visible_index, model_width)
    ).astype(jnp.bfloat16)
    first_inputs = first_inputs.reshape(micro_count, mb_rows, model_width)
    out_grads = grads_full.reshape(micro_count, mb_rows, model_width)
    zeros_full = jnp.zeros((mb_rows, model_width), jnp.bfloat16)
    saved_ticks = []
    received = zeros_full
    for step_index in range(micro_count + 1):
        arriving = received
        own_input = first_inputs[step_index] if step_index < micro_count else zeros_full
        layer_in = jnp.where(is_first, own_input, arriving)
        saved_vals = layer_local(layer_in, norm_scale, weights)
        saved_ticks.append(saved_vals)
        if step_index < micro_count:
            head_part = head_terms(saved_vals[6], weights, model_width)
            mixed = lax.psum(head_part.astype(jnp.bfloat16), "mp").astype(jnp.float32)
            layer_out = (layer_in.astype(jnp.float32) + mixed).astype(jnp.bfloat16)
            received = from_behind(layer_out, "segment", 1)
    back_ticks = []
    for step_index in range(micro_count + 1):
        arriving = received if step_index > 0 else zeros_full
        own_grad = (
            out_grads[micro_count - 1 - step_index] if step_index < micro_count else zeros_full
        )
        d_output = jnp.where(is_first, arriving, own_grad)
        saved_vals = saved_ticks[micro_count - step_index]
        d_project = attention_back(d_output, saved_vals, weights)
        back_ticks.append((d_output, d_project))
        if step_index < micro_count:
            d_terms = feature_terms(d_project, weights, model_width)
            standard, inverse_dev = (saved_vals[1], saved_vals[2])
            summed = lax.psum(d_terms.astype(jnp.bfloat16), "mp").astype(jnp.float32)
            d_input = norm_backward(summed, d_output, standard, inverse_dev, norm_scale)
            received = from_behind(d_input, "segment", -1)
    all_steps = range(micro_count + 1)
    normed_ticks = jnp.stack([saved_ticks[micro_count - step_index][0] for step_index in all_steps])
    attended_ticks = jnp.stack(
        [saved_ticks[micro_count - step_index][6] for step_index in all_steps]
    )
    d_output_ticks = jnp.stack([back_ticks[step_index][0] for step_index in all_steps])
    d_project_ticks = jnp.stack([back_ticks[step_index][1] for step_index in all_steps])
    right_ticks = jnp.concatenate([d_project_ticks, attended_ticks[:, :, None]], axis=2)

    def pick_valid(ticks):
        chosen = jnp.where(is_first, ticks[1:], ticks[:-1])
        return chosen.reshape((micro_count * mb_rows,) + ticks.shape[2:])

    normed_all = pick_valid(normed_ticks)
    d_output_all = pick_valid(d_output_ticks)
    right_all = pick_valid(right_ticks)

    def one_piece(piece_index):
        first_row = piece_index * rows_here
        part_index = first_row // model_width
        col_offset = first_row % model_width
        left_norm = lax.dynamic_slice_in_dim(normed_all, col_offset, rows_here, 1)
        left_grad = lax.dynamic_slice_in_dim(d_output_all, col_offset, rows_here, 1)
        left_side = jnp.where(part_index == 3, left_grad, left_norm)
        right_side = lax.dynamic_index_in_dim(right_all, part_index, 1, keepdims=False)
        return jnp.einsum("tr,tc->rc", left_side, right_side, preferred_element_type=jnp.float32)

    blocks = lax.map(
        one_piece, jnp.arange(rows_here * lax.axis_size("dp") // rows_here, dtype=jnp.int32)
    )
    gradient = lax.psum_scatter(
        blocks.reshape(rows_here * lax.axis_size("dp"), blocks.shape[2]).astype(jnp.bfloat16),
        "dp",
        scatter_dimension=0,
        tiled=True,
    ).astype(jnp.float32)
    new_master, new_first, new_second = adam_update(
        gradient, master_weights[0], first_moment[0], second_moment[0]
    )
    return (new_master[None], new_first[None], new_second[None])

def block_positions(visible_index, model_width, block_width):
    half_width = model_width // 2
    place = lax.axis_index("mp") * block_width + jnp.arange(block_width, dtype=jnp.int32)
    rate = jnp.exp(
        (place % half_width).astype(jnp.float32) * (-2.0 * math.log(10000.0) / model_width)
    )
    angles = visible_index.astype(jnp.float32)[..., None] * rate
    return jnp.where(place < half_width, jnp.sin(angles), jnp.cos(angles))


def gather_tokens(block):
    return lax.all_gather(
        lax.all_gather(block, "dp", axis=0, tiled=True), "mp", axis=1, tiled=True
    )


def exchange_rows(array):
    return lax.all_to_all(array, "dp", 0, 0, tiled=True)


def gather_rows(array):
    return lax.all_gather(array, "dp", axis=0, tiled=True)


def scatter_features(array):
    return lax.psum_scatter(array, "mp", scatter_dimension=1, tiled=True)


def scatter_from_last(array):
    rows = array.shape[0] // lax.axis_size("dp")
    return exchange_rows(array)[-rows:]


def row_sums(array):
    return jnp.sum(lax.all_gather(array, "mp", axis=0), axis=0)


def sum_rows(array):
    peers = lax.axis_size("dp")
    parts = exchange_rows(array).reshape(peers, array.shape[0] // peers, array.shape[1])
    return jnp.sum(parts[: peers - 1].astype(jnp.float32), axis=0)


def split_heads(array, length):
    return array.reshape(-1, length, array.shape[-1] // HD, HD)


def attend(queries, key_rows, values, length):
    queries, key_rows, values = (split_heads(part, length) for part in (queries, key_rows, values))
    scores = jnp.einsum(
        "vqhe,vkhe->vhqk", queries, key_rows, preferred_element_type=jnp.float32
    ) * (1.0 / math.sqrt(HD))
    probs = softmax_rows(scores)
    attended = jnp.einsum(
        "vhqk,vkhe->vqhe",
        probs.astype(jnp.bfloat16),
        values,
        preferred_element_type=jnp.float32,
    )
    return (probs, attended.astype(jnp.bfloat16).reshape(-1, attended.shape[2] * HD))


def attend_back(queries, key_rows, values, probs, d_attended, length):
    queries, key_rows, values, d_attended = (
        split_heads(part, length) for part in (queries, key_rows, values, d_attended)
    )
    d_probs = jnp.einsum(
        "vqhe,vkhe->vhqk", d_attended, values, preferred_element_type=jnp.float32
    )
    d_scores = (
        probs
        * (d_probs - jnp.sum(d_probs * probs, axis=-1, keepdims=True))
        * (1.0 / math.sqrt(HD))
    ).astype(jnp.bfloat16)
    d_queries = jnp.einsum(
        "vhqk,vkhe->vqhe", d_scores, key_rows, preferred_element_type=jnp.float32
    )
    d_keys = jnp.einsum("vhqk,vqhe->vkhe", d_scores, queries, preferred_element_type=jnp.float32)
    d_values = jnp.einsum(
        "vhqk,vqhe->vkhe",
        probs.astype(jnp.bfloat16),
        d_attended,
        preferred_element_type=jnp.float32,
    )
    return tuple(
        part.astype(jnp.bfloat16).reshape(-1, part.shape[2] * HD)
        for part in (d_queries, d_keys, d_values)
    )


def times_weights(left, weights):
    return jnp.dot(left, weights, preferred_element_type=jnp.float32).astype(jnp.bfloat16)


def times_weights_t(left, weights):
    return lax.dot_general(
        left, weights, (((1,), (1,)), ((), ())), preferred_element_type=jnp.float32
    ).astype(jnp.bfloat16)


def still_shards(
    patch_tokens, visible_index, output_grad, norm_gain, master_weights, first_moment, second_moment
):
    peers = lax.axis_size("dp")
    vol_count, length, block_width = patch_tokens.shape
    model_width = block_width * lax.axis_size("mp")
    rows = vol_count * length
    in_first = lax.axis_index("segment") == 0
    holds_out = lax.axis_index("dp") == peers - 1
    norm_scale = norm_gain[0]
    weights = master_weights[0].astype(jnp.bfloat16)
    own_input = (
        patch_tokens.astype(jnp.float32) + block_positions(visible_index, model_width, block_width)
    ).astype(jnp.bfloat16)
    own_input = own_input.reshape(rows, block_width)
    own_grad = output_grad.reshape(rows, block_width)

    def parts_of(array):
        return [array[i * rows : (i + 1) * rows] for i in range(peers)]

    entered = gather_tokens(jnp.where(in_first, own_input, own_grad))
    normed = norm_forward(entered, norm_scale)[0]
    left_first = jnp.where(holds_out, entered, normed)
    q0, k0, v0, _ = parts_of(exchange_rows(times_weights(left_first, weights)))
    probs0, attended0 = attend(q0, k0, v0, length)
    mixed = scatter_from_last(
        scatter_features(times_weights_t(gather_rows(attended0), weights))
    )
    own_out = (own_input.astype(jnp.float32) + mixed.astype(jnp.float32)).astype(jnp.bfloat16)
    own_out = lax.ppermute(own_out, "segment", [(0, 1)])

    middle = gather_tokens(own_out)
    left_second = jnp.where(holds_out, entered, norm_forward(middle, norm_scale)[0])
    q1, k1, v1, da1 = parts_of(exchange_rows(times_weights(left_second, weights)))
    probs1, attended1 = attend(q1, k1, v1, length)
    grads1 = attend_back(q1, k1, v1, probs1, da1, length)
    right_second = exchange_rows(jnp.concatenate(grads1 + (attended1,), axis=0))
    d_normed = sum_rows(scatter_features(times_weights_t(right_second, weights)))

    own_rows = lax.dynamic_slice_in_dim(middle, lax.axis_index("dp") * rows, rows, 0)
    own_cols = lax.axis_index("mp") * block_width
    _, standard, inverse_dev = norm_forward(own_rows, norm_scale)
    standard = lax.dynamic_slice_in_dim(standard, own_cols, block_width, 1)
    scaled = d_normed * lax.dynamic_slice_in_dim(norm_scale, own_cols, block_width, 0)
    sums = row_sums(
        jnp.stack([jnp.sum(scaled, axis=-1), jnp.sum(scaled * standard, axis=-1)])
    ) * (1.0 / model_width)
    inner = scaled - sums[0][:, None] - standard * sums[1][:, None]
    own_d = (own_grad.astype(jnp.float32) + inner * inverse_dev).astype(jnp.bfloat16)
    own_d = lax.ppermute(own_d, "segment", [(1, 0)])

    returned = gather_tokens(own_d)
    da0 = scatter_from_last(times_weights(returned, weights))
    grads0 = attend_back(q0, k0, v0, probs0, da0, length)
    right_first = exchange_rows(jnp.concatenate(grads0 + (attended0,), axis=0))

    left_first = jnp.where(holds_out, returned, normed)
    left_side = jnp.where(in_first, left_first, left_second)
    right_side = jnp.where(in_first, right_first, right_second)
    gradient = lax.dot_general(
        left_side, right_side, (((0,), (0,)), ((), ())), preferred_element_type=jnp.float32
    )
    new_master, new_first, new_second = adam_update(
        gradient, master_weights[0], first_moment[0], second_moment[0]
    )
    return (new_master[None], new_first[None], new_second[None])


def section_step(*arrays):
    model_width = arrays[0].shape[2] * lax.axis_size("mp")
    if arrays[4].shape[1] == model_width and lax.axis_size("dp") == 4:
        return still_shards(*arrays)
    return shards(*arrays)


def solution(mesh):
    placed = (
        P("dp", None, "mp"),
        P("dp", None),
        P("dp", None, "mp"),
        P("segment", None),
        P("segment", "dp", "mp"),
        P("segment", "dp", "mp"),
        P("segment", "dp", "mp"),
    )
    return jax.shard_map(
        section_step,
        mesh=mesh,
        in_specs=placed,
        out_specs=(P("segment", "dp", "mp"), P("segment", "dp", "mp"), P("segment", "dp", "mp")),
        check_vma=False,
    )
```

```python
import functools
import math

import jax
import jax.numpy as jnp
from jax import lax
from jax.experimental import pallas as pl
from jax.experimental.pallas import tpu as pltpu
from jax.sharding import PartitionSpec as P

HD = 128
MB_VOLS = 2


beta_one = 0.9
beta_two = 0.95
learn_rate = 0.01
decay_rate = 0.1
adam_eps = 1e-08
norm_eps = 1e-05
step_count = 10


def from_behind(array, axis, by):
    peers = lax.axis_size(axis)
    pairs = [(i, i + by) for i in range(peers) if 0 <= i + by < peers]
    return lax.ppermute(array, axis, pairs)


def position_table(visible_index, model_width):
    half_width = model_width // 2
    angle_rate = jnp.exp(
        jnp.arange(half_width, dtype=jnp.float32) * (-2.0 * math.log(10000.0) / model_width)
    )
    angles = visible_index.astype(jnp.float32)[..., None] * angle_rate
    return jnp.concatenate([jnp.sin(angles), jnp.cos(angles)], axis=-1)


def norm_forward(hidden, norm_scale):
    values = hidden.astype(jnp.float32)
    centred = values - jnp.mean(values, axis=-1, keepdims=True)
    inverse_dev = lax.rsqrt(jnp.mean(centred * centred, axis=-1, keepdims=True) + norm_eps)
    standard = centred * inverse_dev
    return ((standard * norm_scale).astype(jnp.bfloat16), standard, inverse_dev)


def norm_backward(d_normed, d_output, standard, inverse_dev, norm_scale):
    scaled = d_normed * norm_scale
    inner = (
        scaled
        - jnp.mean(scaled, axis=-1, keepdims=True)
        - standard * jnp.mean(scaled * standard, axis=-1, keepdims=True)
    )
    return (d_output.astype(jnp.float32) + inner * inverse_dev).astype(jnp.bfloat16)


def softmax_rows(scores):
    lifted = jnp.exp(scores - jnp.max(scores, axis=-1, keepdims=True))
    return lifted / jnp.sum(lifted, axis=-1, keepdims=True)


def rounded(values):
    return lax.optimization_barrier(values.astype(jnp.bfloat16)).astype(jnp.float32)


def adam_update(gradient, master, first_moment, second_moment):
    new_first = beta_one * first_moment + (1.0 - beta_one) * gradient
    new_second = beta_two * second_moment + (1.0 - beta_two) * gradient * gradient
    direction = (
        new_first
        / (1.0 - beta_one**step_count)
        / (jnp.sqrt(new_second / (1.0 - beta_two**step_count)) + adam_eps)
    )
    new_master = master - learn_rate * (direction + decay_rate * master)
    return (new_master, new_first, new_second)


def layer_local(layer_in, norm_scale, weights):
    row_count, model_width = layer_in.shape
    col_count = weights.shape[1]
    head_count = col_count // HD
    length = row_count // MB_VOLS
    normed, standard, inverse_dev = norm_forward(layer_in, norm_scale)
    triple = weights[: 3 * model_width].reshape(3, model_width, col_count)
    project = jnp.einsum("nd,sdc->nsc", normed, triple, preferred_element_type=jnp.float32).astype(
        jnp.bfloat16
    )
    shaped = project.reshape(MB_VOLS, length, 3, head_count, HD)
    scores = jnp.einsum(
        "vqhe,vkhe->vhqk", shaped[:, :, 0], shaped[:, :, 1], preferred_element_type=jnp.float32
    ) * (1.0 / math.sqrt(HD))
    softmaxed = softmax_rows(scores)
    probs_half = softmaxed.astype(jnp.bfloat16)
    attended = jnp.einsum(
        "vhqk,vkhe->vqhe", probs_half, shaped[:, :, 2], preferred_element_type=jnp.float32
    )
    attended = attended.astype(jnp.bfloat16).reshape(row_count, col_count)
    return (normed, standard, inverse_dev, project, softmaxed, probs_half, attended)


def head_terms(attended, weights, model_width):
    return rounded(
        jnp.einsum(
            "nc,dc->nd", attended, weights[3 * model_width :], preferred_element_type=jnp.float32
        )
    )


def attention_back(d_output, saved_vals, weights):
    project, softmaxed, probs_half = (saved_vals[3], saved_vals[4], saved_vals[5])
    row_count, model_width = d_output.shape
    col_count = weights.shape[1]
    head_count = col_count // HD
    length = row_count // MB_VOLS
    shaped = project.reshape(MB_VOLS, length, 3, head_count, HD)
    d_attended = jnp.einsum(
        "nd,dc->nc", d_output, weights[3 * model_width :], preferred_element_type=jnp.float32
    )
    d_attended = d_attended.astype(jnp.bfloat16).reshape(MB_VOLS, length, head_count, HD)
    d_probs = jnp.einsum(
        "vqhe,vkhe->vhqk", d_attended, shaped[:, :, 2], preferred_element_type=jnp.float32
    )
    d_scores = (
        softmaxed
        * (d_probs - jnp.sum(d_probs * softmaxed, axis=-1, keepdims=True))
        * (1.0 / math.sqrt(HD))
    ).astype(jnp.bfloat16)
    d_queries = jnp.einsum(
        "vhqk,vkhe->vqhe", d_scores, shaped[:, :, 1], preferred_element_type=jnp.float32
    ).astype(jnp.bfloat16)
    d_keys = jnp.einsum(
        "vhqk,vqhe->vkhe", d_scores, shaped[:, :, 0], preferred_element_type=jnp.float32
    ).astype(jnp.bfloat16)
    d_values = jnp.einsum(
        "vhqk,vqhe->vkhe", probs_half, d_attended, preferred_element_type=jnp.float32
    ).astype(jnp.bfloat16)
    return jnp.stack([d_queries, d_keys, d_values], axis=2).reshape(row_count, 3, col_count)


def feature_terms(d_project, weights, model_width):
    col_count = weights.shape[1]
    triple = weights[: 3 * model_width].reshape(3, model_width, col_count)
    return rounded(jnp.einsum("nsc,sdc->nd", d_project, triple, preferred_element_type=jnp.float32))


def shards(
    patch_tokens, visible_index, output_grad, norm_gain, master_weights, first_moment, second_moment
):
    model_width = patch_tokens.shape[2] * lax.axis_size("mp")
    rows_here = master_weights.shape[1]
    is_first = lax.axis_index("segment") == 0
    norm_scale = norm_gain[0]
    weights = lax.all_gather(master_weights[0].astype(jnp.bfloat16), "dp", axis=0, tiled=True)
    tokens_full, grads_full = (
        lax.all_gather(patch_tokens, "mp", axis=2, tiled=True),
        lax.all_gather(output_grad, "mp", axis=2, tiled=True),
    )
    vol_count, length = visible_index.shape
    micro_count = vol_count // MB_VOLS
    mb_rows = MB_VOLS * length
    first_inputs = (
        tokens_full.astype(jnp.float32) + position_table(visible_index, model_width)
    ).astype(jnp.bfloat16)
    first_inputs = first_inputs.reshape(micro_count, mb_rows, model_width)
    out_grads = grads_full.reshape(micro_count, mb_rows, model_width)
    zeros_full = jnp.zeros((mb_rows, model_width), jnp.bfloat16)
    saved_ticks = []
    received = zeros_full
    for step_index in range(micro_count + 1):
        arriving = received
        own_input = first_inputs[step_index] if step_index < micro_count else zeros_full
        layer_in = jnp.where(is_first, own_input, arriving)
        saved_vals = layer_local(layer_in, norm_scale, weights)
        saved_ticks.append(saved_vals)
        if step_index < micro_count:
            head_part = head_terms(saved_vals[6], weights, model_width)
            mixed = lax.psum(head_part.astype(jnp.bfloat16), "mp").astype(jnp.float32)
            layer_out = (layer_in.astype(jnp.float32) + mixed).astype(jnp.bfloat16)
            received = from_behind(layer_out, "segment", 1)
    back_ticks = []
    for step_index in range(micro_count + 1):
        arriving = received if step_index > 0 else zeros_full
        own_grad = (
            out_grads[micro_count - 1 - step_index] if step_index < micro_count else zeros_full
        )
        d_output = jnp.where(is_first, arriving, own_grad)
        saved_vals = saved_ticks[micro_count - step_index]
        d_project = attention_back(d_output, saved_vals, weights)
        back_ticks.append((d_output, d_project))
        if step_index < micro_count:
            d_terms = feature_terms(d_project, weights, model_width)
            standard, inverse_dev = (saved_vals[1], saved_vals[2])
            summed = lax.psum(d_terms.astype(jnp.bfloat16), "mp").astype(jnp.float32)
            d_input = norm_backward(summed, d_output, standard, inverse_dev, norm_scale)
            received = from_behind(d_input, "segment", -1)
    all_steps = range(micro_count + 1)
    normed_ticks = jnp.stack([saved_ticks[micro_count - step_index][0] for step_index in all_steps])
    attended_ticks = jnp.stack(
        [saved_ticks[micro_count - step_index][6] for step_index in all_steps]
    )
    d_output_ticks = jnp.stack([back_ticks[step_index][0] for step_index in all_steps])
    d_project_ticks = jnp.stack([back_ticks[step_index][1] for step_index in all_steps])
    right_ticks = jnp.concatenate([d_project_ticks, attended_ticks[:, :, None]], axis=2)

    def pick_valid(ticks):
        chosen = jnp.where(is_first, ticks[1:], ticks[:-1])
        return chosen.reshape((micro_count * mb_rows,) + ticks.shape[2:])

    normed_all = pick_valid(normed_ticks)
    d_output_all = pick_valid(d_output_ticks)
    right_all = pick_valid(right_ticks)

    def one_piece(piece_index):
        first_row = piece_index * rows_here
        part_index = first_row // model_width
        col_offset = first_row % model_width
        left_norm = lax.dynamic_slice_in_dim(normed_all, col_offset, rows_here, 1)
        left_grad = lax.dynamic_slice_in_dim(d_output_all, col_offset, rows_here, 1)
        left_side = jnp.where(part_index == 3, left_grad, left_norm)
        right_side = lax.dynamic_index_in_dim(right_all, part_index, 1, keepdims=False)
        return jnp.einsum("tr,tc->rc", left_side, right_side, preferred_element_type=jnp.float32)

    blocks = lax.map(
        one_piece, jnp.arange(rows_here * lax.axis_size("dp") // rows_here, dtype=jnp.int32)
    )
    gradient = lax.psum_scatter(
        blocks.reshape(rows_here * lax.axis_size("dp"), blocks.shape[2]).astype(jnp.bfloat16),
        "dp",
        scatter_dimension=0,
        tiled=True,
    ).astype(jnp.float32)
    new_master, new_first, new_second = adam_update(
        gradient, master_weights[0], first_moment[0], second_moment[0]
    )
    return (new_master[None], new_first[None], new_second[None])

def block_positions(visible_index, model_width, block_width):
    half_width = model_width // 2
    place = lax.axis_index("mp") * block_width + jnp.arange(block_width, dtype=jnp.int32)
    rate = jnp.exp(
        (place % half_width).astype(jnp.float32) * (-2.0 * math.log(10000.0) / model_width)
    )
    angles = visible_index.astype(jnp.float32)[..., None] * rate
    return jnp.where(place < half_width, jnp.sin(angles), jnp.cos(angles))


def greet(partners):
    barrier = pltpu.get_barrier_semaphore()
    for partner in partners:
        pl.semaphore_signal(
            barrier, inc=1, device_id=partner, device_id_type=pl.DeviceIdType.MESH
        )
    pl.semaphore_wait(barrier, len(partners))


def push(source, target, send_sem, recv_sem, partner):
    return pltpu.make_async_remote_copy(
        src_ref=source,
        dst_ref=target,
        send_sem=send_sem,
        recv_sem=recv_sem,
        device_id=partner,
        device_id_type=pl.DeviceIdType.MESH,
    )


def in_vmem(kernel, operand, out_shape, scratch, collective_id):
    return pl.pallas_call(
        kernel,
        out_shape=out_shape,
        in_specs=[pl.BlockSpec(memory_space=pltpu.VMEM)],
        out_specs=pl.BlockSpec(memory_space=pltpu.VMEM),
        scratch_shapes=scratch,
        compiler_params=pltpu.CompilerParams(
            collective_id=collective_id, has_side_effects=True, vmem_limit_bytes=40 * 2**20
        ),
    )(operand)


def mesh_partners(peers):
    row, col = lax.axis_index("dp"), lax.axis_index("mp")
    along = [{"dp": lax.rem(row + step, peers)} for step in range(1, peers)]
    across = {"mp": lax.rem(col + 2, 4)}
    beside = {"mp": col + 1 - 2 * lax.rem(col, 2)}
    return (along, across, beside)


def gather_kernel(peers, x_ref, o_ref, z_send, z_recv, y_send, y_recv, c_send, c_recv):
    rows, width = x_ref.shape
    row, col = lax.axis_index("dp"), lax.axis_index("mp")
    along, across, beside = mesh_partners(peers)
    greet(along + [across, beside])

    def place(step, owner):
        source = lax.rem(row - step + peers, peers)
        return o_ref.at[
            pl.ds(pl.multiple_of(source * rows, rows), rows),
            pl.ds(pl.multiple_of(owner * width, width), width),
        ]

    over = lax.rem(col + 2, 4)
    along_copies = [
        push(x_ref, place(0, col), z_send.at[step], z_recv.at[step], along[step])
        for step in range(peers - 1)
    ]
    for copy in along_copies:
        copy.start()
    across_copies, beside_copies = [], []
    for step in range(peers):
        source = x_ref
        if step > 0:
            along_copies[step - 1].wait_recv()
            source = place(step, col)
        across_copies.append(
            push(source, place(step, col), y_send.at[step], y_recv.at[step], across)
        )
        across_copies[-1].start()
        beside_copies.append(
            push(source, place(step, col), c_send.at[step], c_recv.at[step], beside)
        )
        beside_copies[-1].start()
    own_rows = pl.ds(pl.multiple_of(row * rows, rows), rows)
    o_ref[own_rows, pl.ds(pl.multiple_of(col * width, width), width)] = x_ref[...]
    for step in range(peers):
        across_copies[step].wait_recv()
        at = peers + step
        beside_copies.append(
            push(place(step, over), place(step, over), c_send.at[at], c_recv.at[at], beside)
        )
        beside_copies[-1].start()
    for copy in beside_copies:
        copy.wait_recv()
    for copy in along_copies + across_copies + beside_copies:
        copy.wait_send()


def gather_tokens(block):
    peers = lax.axis_size("dp")
    shape = (block.shape[0] * peers, block.shape[1] * 4)
    dma = pltpu.SemaphoreType.DMA
    return in_vmem(
        functools.partial(gather_kernel, peers),
        block,
        jax.ShapeDtypeStruct(shape, block.dtype),
        [dma((peers - 1,))] * 2 + [dma((peers,))] * 2 + [dma((2 * peers,))] * 2,
        0,
    )


def exchange_kernel(peers, x_ref, o_ref, send, recv):
    rows = x_ref.shape[0] // peers
    row = lax.axis_index("dp")
    along = mesh_partners(peers)[0]
    greet(along)
    own = pl.ds(pl.multiple_of(row * rows, rows), rows)
    copies = []
    for step in range(1, peers):
        other = lax.rem(row + step, peers)
        theirs = pl.ds(pl.multiple_of(other * rows, rows), rows)
        copies.append(
            push(
                x_ref.at[theirs], o_ref.at[own], send.at[step - 1], recv.at[step - 1], along[step - 1]
            )
        )
        copies[-1].start()
    o_ref[own] = x_ref[own]
    for copy in copies:
        copy.wait()


def exchange_rows(array):
    peers = lax.axis_size("dp")
    return in_vmem(
        functools.partial(exchange_kernel, peers),
        array,
        jax.ShapeDtypeStruct(array.shape, array.dtype),
        [pltpu.SemaphoreType.DMA((peers - 1,))] * 2,
        1 if array.shape[1] % 768 else 2,
    )


def spread_kernel(peers, x_ref, o_ref, send, recv):
    rows = x_ref.shape[0]
    row = lax.axis_index("dp")
    along = mesh_partners(peers)[0]
    greet(along)
    own = pl.ds(pl.multiple_of(row * rows, rows), rows)
    copies = [
        push(x_ref, o_ref.at[own], send.at[step], recv.at[step], along[step])
        for step in range(peers - 1)
    ]
    for copy in copies:
        copy.start()
    o_ref[own] = x_ref[...]
    for copy in copies:
        copy.wait()


def gather_rows(array):
    peers = lax.axis_size("dp")
    return in_vmem(
        functools.partial(spread_kernel, peers),
        array,
        jax.ShapeDtypeStruct((array.shape[0] * peers, array.shape[1]), array.dtype),
        [pltpu.SemaphoreType.DMA((peers - 1,))] * 2,
        3,
    )


def scatter_kernel(
    peers, x_ref, o_ref, came, passed, landed, c_send, c_recv, y_send, y_recv
):
    width = x_ref.shape[1] // 4
    rows = x_ref.shape[0] // peers
    col = lax.axis_index("mp")
    _, across, beside = mesh_partners(peers)
    greet([across, beside])
    next_to = col + 1 - 2 * lax.rem(col, 2)
    over = lax.rem(col + 2, 4)
    over_next = lax.rem(next_to + 2, 4)

    def piece(step, owner):
        return (
            pl.ds(step * rows, rows),
            pl.ds(pl.multiple_of(owner * width, width), width),
        )

    far, near = [], []
    for step in range(peers):
        for slot, owner, copies in ((0, over_next, far), (1, next_to, near)):
            at = slot * peers + step
            copies.append(
                push(
                    x_ref.at[piece(step, owner)],
                    came.at[slot, pl.ds(step * rows, rows)],
                    c_send.at[at],
                    c_recv.at[at],
                    beside,
                )
            )
            if slot == 0:
                copies[-1].start()
    for copy in near:
        copy.start()
    across_copies = []
    for step in range(peers):
        here = pl.ds(step * rows, rows)
        far[step].wait_recv()
        passed[here] = (
            x_ref[piece(step, over)].astype(jnp.float32) + came[0, here].astype(jnp.float32)
        ).astype(jnp.bfloat16)
        across_copies.append(
            push(passed.at[here], landed.at[here], y_send.at[step], y_recv.at[step], across)
        )
        across_copies[-1].start()
    for step in range(peers):
        here = pl.ds(step * rows, rows)
        near[step].wait_recv()
        across_copies[step].wait_recv()
        o_ref[here] = (
            x_ref[piece(step, col)].astype(jnp.float32)
            + came[1, here].astype(jnp.float32)
            + landed[here].astype(jnp.float32)
        ).astype(jnp.bfloat16)
    for copy in far + near + across_copies:
        copy.wait_send()


def scatter_features(array):
    peers = lax.axis_size("dp")
    shape = (array.shape[0], array.shape[1] // 4)
    dma = pltpu.SemaphoreType.DMA
    return in_vmem(
        functools.partial(scatter_kernel, peers),
        array,
        jax.ShapeDtypeStruct(shape, array.dtype),
        [
            pltpu.VMEM((2,) + shape, jnp.bfloat16),
            pltpu.VMEM(shape, jnp.bfloat16),
            pltpu.VMEM(shape, jnp.bfloat16),
        ]
        + [dma((2 * peers,))] * 2
        + [dma((peers,))] * 2,
        4,
    )


def scatter_from_last(array):
    rows = array.shape[0] // lax.axis_size("dp")
    return exchange_rows(array)[-rows:]


def row_sums(array):
    return jnp.sum(lax.all_gather(array, "mp", axis=0), axis=0)


def sum_rows(array):
    peers = lax.axis_size("dp")
    parts = exchange_rows(array).reshape(peers, array.shape[0] // peers, array.shape[1])
    return jnp.sum(parts[: peers - 1].astype(jnp.float32), axis=0)


def split_heads(array, length):
    return array.reshape(-1, length, array.shape[-1] // HD, HD)


def attend(queries, key_rows, values, length):
    queries, key_rows, values = (split_heads(part, length) for part in (queries, key_rows, values))
    scores = jnp.einsum(
        "vqhe,vkhe->vhqk", queries, key_rows, preferred_element_type=jnp.float32
    ) * (1.0 / math.sqrt(HD))
    probs = softmax_rows(scores)
    attended = jnp.einsum(
        "vhqk,vkhe->vqhe",
        probs.astype(jnp.bfloat16),
        values,
        preferred_element_type=jnp.float32,
    )
    return (probs, attended.astype(jnp.bfloat16).reshape(-1, attended.shape[2] * HD))


def attend_back(queries, key_rows, values, probs, d_attended, length):
    queries, key_rows, values, d_attended = (
        split_heads(part, length) for part in (queries, key_rows, values, d_attended)
    )
    d_probs = jnp.einsum(
        "vqhe,vkhe->vhqk", d_attended, values, preferred_element_type=jnp.float32
    )
    d_scores = (
        probs
        * (d_probs - jnp.sum(d_probs * probs, axis=-1, keepdims=True))
        * (1.0 / math.sqrt(HD))
    ).astype(jnp.bfloat16)
    d_queries = jnp.einsum(
        "vhqk,vkhe->vqhe", d_scores, key_rows, preferred_element_type=jnp.float32
    )
    d_keys = jnp.einsum("vhqk,vqhe->vkhe", d_scores, queries, preferred_element_type=jnp.float32)
    d_values = jnp.einsum(
        "vhqk,vqhe->vkhe",
        probs.astype(jnp.bfloat16),
        d_attended,
        preferred_element_type=jnp.float32,
    )
    return tuple(
        part.astype(jnp.bfloat16).reshape(-1, part.shape[2] * HD)
        for part in (d_queries, d_keys, d_values)
    )


def times_weights(left, weights):
    return jnp.dot(left, weights, preferred_element_type=jnp.float32).astype(jnp.bfloat16)


def times_weights_t(left, weights):
    return lax.dot_general(
        left, weights, (((1,), (1,)), ((), ())), preferred_element_type=jnp.float32
    ).astype(jnp.bfloat16)


def still_shards(
    patch_tokens, visible_index, output_grad, norm_gain, master_weights, first_moment, second_moment
):
    peers = lax.axis_size("dp")
    vol_count, length, block_width = patch_tokens.shape
    model_width = block_width * lax.axis_size("mp")
    rows = vol_count * length
    in_first = lax.axis_index("segment") == 0
    holds_out = lax.axis_index("dp") == peers - 1
    norm_scale = norm_gain[0]
    weights = master_weights[0].astype(jnp.bfloat16)
    own_input = (
        patch_tokens.astype(jnp.float32) + block_positions(visible_index, model_width, block_width)
    ).astype(jnp.bfloat16)
    own_input = own_input.reshape(rows, block_width)
    own_grad = output_grad.reshape(rows, block_width)

    def parts_of(array):
        return [array[i * rows : (i + 1) * rows] for i in range(peers)]

    entered = gather_tokens(jnp.where(in_first, own_input, own_grad))
    normed = norm_forward(entered, norm_scale)[0]
    left_first = jnp.where(holds_out, entered, normed)
    q0, k0, v0, _ = parts_of(exchange_rows(times_weights(left_first, weights)))
    probs0, attended0 = attend(q0, k0, v0, length)
    mixed = scatter_from_last(
        scatter_features(times_weights_t(gather_rows(attended0), weights))
    )
    own_out = (own_input.astype(jnp.float32) + mixed.astype(jnp.float32)).astype(jnp.bfloat16)
    own_out = lax.ppermute(own_out, "segment", [(0, 1)])

    middle = gather_tokens(own_out)
    left_second = jnp.where(holds_out, entered, norm_forward(middle, norm_scale)[0])
    q1, k1, v1, da1 = parts_of(exchange_rows(times_weights(left_second, weights)))
    probs1, attended1 = attend(q1, k1, v1, length)
    grads1 = attend_back(q1, k1, v1, probs1, da1, length)
    right_second = exchange_rows(jnp.concatenate(grads1 + (attended1,), axis=0))
    d_normed = sum_rows(scatter_features(times_weights_t(right_second, weights)))

    own_rows = lax.dynamic_slice_in_dim(middle, lax.axis_index("dp") * rows, rows, 0)
    own_cols = lax.axis_index("mp") * block_width
    _, standard, inverse_dev = norm_forward(own_rows, norm_scale)
    standard = lax.dynamic_slice_in_dim(standard, own_cols, block_width, 1)
    scaled = d_normed * lax.dynamic_slice_in_dim(norm_scale, own_cols, block_width, 0)
    sums = row_sums(
        jnp.stack([jnp.sum(scaled, axis=-1), jnp.sum(scaled * standard, axis=-1)])
    ) * (1.0 / model_width)
    inner = scaled - sums[0][:, None] - standard * sums[1][:, None]
    own_d = (own_grad.astype(jnp.float32) + inner * inverse_dev).astype(jnp.bfloat16)
    own_d = lax.ppermute(own_d, "segment", [(1, 0)])

    returned = gather_tokens(own_d)
    da0 = scatter_from_last(times_weights(returned, weights))
    grads0 = attend_back(q0, k0, v0, probs0, da0, length)
    right_first = exchange_rows(jnp.concatenate(grads0 + (attended0,), axis=0))

    left_first = jnp.where(holds_out, returned, normed)
    left_side = jnp.where(in_first, left_first, left_second)
    right_side = jnp.where(in_first, right_first, right_second)
    gradient = lax.dot_general(
        left_side, right_side, (((0,), (0,)), ((), ())), preferred_element_type=jnp.float32
    )
    new_master, new_first, new_second = adam_update(
        gradient, master_weights[0], first_moment[0], second_moment[0]
    )
    return (new_master[None], new_first[None], new_second[None])


def section_step(*arrays):
    model_width = arrays[0].shape[2] * lax.axis_size("mp")
    sizes = tuple(lax.axis_size(axis) for axis in ("segment", "dp", "mp"))
    if arrays[4].shape[1] == model_width and sizes == (2, 4, 4):
        return still_shards(*arrays)
    return shards(*arrays)


def solution(mesh):
    placed = (
        P("dp", None, "mp"),
        P("dp", None),
        P("dp", None, "mp"),
        P("segment", None),
        P("segment", "dp", "mp"),
        P("segment", "dp", "mp"),
        P("segment", "dp", "mp"),
    )
    return jax.shard_map(
        section_step,
        mesh=mesh,
        in_specs=placed,
        out_specs=(P("segment", "dp", "mp"), P("segment", "dp", "mp"), P("segment", "dp", "mp")),
        check_vma=False,
    )
```

```python
import functools
import math

import jax
import jax.numpy as jnp
from jax import lax
from jax.experimental import pallas as pl
from jax.experimental.pallas import tpu as pltpu
from jax.sharding import PartitionSpec as P

HD = 128
MB_VOLS = 2


beta_one = 0.9
beta_two = 0.95
learn_rate = 0.01
decay_rate = 0.1
adam_eps = 1e-08
norm_eps = 1e-05
step_count = 10


def from_behind(array, axis, by):
    peers = lax.axis_size(axis)
    pairs = [(i, i + by) for i in range(peers) if 0 <= i + by < peers]
    return lax.ppermute(array, axis, pairs)


def position_table(visible_index, model_width):
    half_width = model_width // 2
    angle_rate = jnp.exp(
        jnp.arange(half_width, dtype=jnp.float32) * (-2.0 * math.log(10000.0) / model_width)
    )
    angles = visible_index.astype(jnp.float32)[..., None] * angle_rate
    return jnp.concatenate([jnp.sin(angles), jnp.cos(angles)], axis=-1)


def norm_forward(hidden, norm_scale):
    values = hidden.astype(jnp.float32)
    centred = values - jnp.mean(values, axis=-1, keepdims=True)
    inverse_dev = lax.rsqrt(jnp.mean(centred * centred, axis=-1, keepdims=True) + norm_eps)
    standard = centred * inverse_dev
    return ((standard * norm_scale).astype(jnp.bfloat16), standard, inverse_dev)


def norm_backward(d_normed, d_output, standard, inverse_dev, norm_scale):
    scaled = d_normed * norm_scale
    inner = (
        scaled
        - jnp.mean(scaled, axis=-1, keepdims=True)
        - standard * jnp.mean(scaled * standard, axis=-1, keepdims=True)
    )
    return (d_output.astype(jnp.float32) + inner * inverse_dev).astype(jnp.bfloat16)


def softmax_rows(scores):
    lifted = jnp.exp(scores - jnp.max(scores, axis=-1, keepdims=True))
    return lifted / jnp.sum(lifted, axis=-1, keepdims=True)


def rounded(values):
    return lax.optimization_barrier(values.astype(jnp.bfloat16)).astype(jnp.float32)


def adam_update(gradient, master, first_moment, second_moment):
    new_first = beta_one * first_moment + (1.0 - beta_one) * gradient
    new_second = beta_two * second_moment + (1.0 - beta_two) * gradient * gradient
    direction = (
        new_first
        / (1.0 - beta_one**step_count)
        / (jnp.sqrt(new_second / (1.0 - beta_two**step_count)) + adam_eps)
    )
    new_master = master - learn_rate * (direction + decay_rate * master)
    return (new_master, new_first, new_second)


def layer_local(layer_in, norm_scale, weights):
    row_count, model_width = layer_in.shape
    col_count = weights.shape[1]
    head_count = col_count // HD
    length = row_count // MB_VOLS
    normed, standard, inverse_dev = norm_forward(layer_in, norm_scale)
    triple = weights[: 3 * model_width].reshape(3, model_width, col_count)
    project = jnp.einsum("nd,sdc->nsc", normed, triple, preferred_element_type=jnp.float32).astype(
        jnp.bfloat16
    )
    shaped = project.reshape(MB_VOLS, length, 3, head_count, HD)
    scores = jnp.einsum(
        "vqhe,vkhe->vhqk", shaped[:, :, 0], shaped[:, :, 1], preferred_element_type=jnp.float32
    ) * (1.0 / math.sqrt(HD))
    softmaxed = softmax_rows(scores)
    probs_half = softmaxed.astype(jnp.bfloat16)
    attended = jnp.einsum(
        "vhqk,vkhe->vqhe", probs_half, shaped[:, :, 2], preferred_element_type=jnp.float32
    )
    attended = attended.astype(jnp.bfloat16).reshape(row_count, col_count)
    return (normed, standard, inverse_dev, project, softmaxed, probs_half, attended)


def head_terms(attended, weights, model_width):
    return rounded(
        jnp.einsum(
            "nc,dc->nd", attended, weights[3 * model_width :], preferred_element_type=jnp.float32
        )
    )


def attention_back(d_output, saved_vals, weights):
    project, softmaxed, probs_half = (saved_vals[3], saved_vals[4], saved_vals[5])
    row_count, model_width = d_output.shape
    col_count = weights.shape[1]
    head_count = col_count // HD
    length = row_count // MB_VOLS
    shaped = project.reshape(MB_VOLS, length, 3, head_count, HD)
    d_attended = jnp.einsum(
        "nd,dc->nc", d_output, weights[3 * model_width :], preferred_element_type=jnp.float32
    )
    d_attended = d_attended.astype(jnp.bfloat16).reshape(MB_VOLS, length, head_count, HD)
    d_probs = jnp.einsum(
        "vqhe,vkhe->vhqk", d_attended, shaped[:, :, 2], preferred_element_type=jnp.float32
    )
    d_scores = (
        softmaxed
        * (d_probs - jnp.sum(d_probs * softmaxed, axis=-1, keepdims=True))
        * (1.0 / math.sqrt(HD))
    ).astype(jnp.bfloat16)
    d_queries = jnp.einsum(
        "vhqk,vkhe->vqhe", d_scores, shaped[:, :, 1], preferred_element_type=jnp.float32
    ).astype(jnp.bfloat16)
    d_keys = jnp.einsum(
        "vhqk,vqhe->vkhe", d_scores, shaped[:, :, 0], preferred_element_type=jnp.float32
    ).astype(jnp.bfloat16)
    d_values = jnp.einsum(
        "vhqk,vqhe->vkhe", probs_half, d_attended, preferred_element_type=jnp.float32
    ).astype(jnp.bfloat16)
    return jnp.stack([d_queries, d_keys, d_values], axis=2).reshape(row_count, 3, col_count)


def feature_terms(d_project, weights, model_width):
    col_count = weights.shape[1]
    triple = weights[: 3 * model_width].reshape(3, model_width, col_count)
    return rounded(jnp.einsum("nsc,sdc->nd", d_project, triple, preferred_element_type=jnp.float32))


def shards(
    patch_tokens, visible_index, output_grad, norm_gain, master_weights, first_moment, second_moment
):
    model_width = patch_tokens.shape[2] * lax.axis_size("mp")
    rows_here = master_weights.shape[1]
    is_first = lax.axis_index("segment") == 0
    norm_scale = norm_gain[0]
    weights = lax.all_gather(master_weights[0].astype(jnp.bfloat16), "dp", axis=0, tiled=True)
    tokens_full, grads_full = (
        lax.all_gather(patch_tokens, "mp", axis=2, tiled=True),
        lax.all_gather(output_grad, "mp", axis=2, tiled=True),
    )
    vol_count, length = visible_index.shape
    micro_count = vol_count // MB_VOLS
    mb_rows = MB_VOLS * length
    first_inputs = (
        tokens_full.astype(jnp.float32) + position_table(visible_index, model_width)
    ).astype(jnp.bfloat16)
    first_inputs = first_inputs.reshape(micro_count, mb_rows, model_width)
    out_grads = grads_full.reshape(micro_count, mb_rows, model_width)
    zeros_full = jnp.zeros((mb_rows, model_width), jnp.bfloat16)
    saved_ticks = []
    received = zeros_full
    for step_index in range(micro_count + 1):
        arriving = received
        own_input = first_inputs[step_index] if step_index < micro_count else zeros_full
        layer_in = jnp.where(is_first, own_input, arriving)
        saved_vals = layer_local(layer_in, norm_scale, weights)
        saved_ticks.append(saved_vals)
        if step_index < micro_count:
            head_part = head_terms(saved_vals[6], weights, model_width)
            mixed = lax.psum(head_part.astype(jnp.bfloat16), "mp").astype(jnp.float32)
            layer_out = (layer_in.astype(jnp.float32) + mixed).astype(jnp.bfloat16)
            received = from_behind(layer_out, "segment", 1)
    back_ticks = []
    for step_index in range(micro_count + 1):
        arriving = received if step_index > 0 else zeros_full
        own_grad = (
            out_grads[micro_count - 1 - step_index] if step_index < micro_count else zeros_full
        )
        d_output = jnp.where(is_first, arriving, own_grad)
        saved_vals = saved_ticks[micro_count - step_index]
        d_project = attention_back(d_output, saved_vals, weights)
        back_ticks.append((d_output, d_project))
        if step_index < micro_count:
            d_terms = feature_terms(d_project, weights, model_width)
            standard, inverse_dev = (saved_vals[1], saved_vals[2])
            summed = lax.psum(d_terms.astype(jnp.bfloat16), "mp").astype(jnp.float32)
            d_input = norm_backward(summed, d_output, standard, inverse_dev, norm_scale)
            received = from_behind(d_input, "segment", -1)
    all_steps = range(micro_count + 1)
    normed_ticks = jnp.stack([saved_ticks[micro_count - step_index][0] for step_index in all_steps])
    attended_ticks = jnp.stack(
        [saved_ticks[micro_count - step_index][6] for step_index in all_steps]
    )
    d_output_ticks = jnp.stack([back_ticks[step_index][0] for step_index in all_steps])
    d_project_ticks = jnp.stack([back_ticks[step_index][1] for step_index in all_steps])
    right_ticks = jnp.concatenate([d_project_ticks, attended_ticks[:, :, None]], axis=2)

    def pick_valid(ticks):
        chosen = jnp.where(is_first, ticks[1:], ticks[:-1])
        return chosen.reshape((micro_count * mb_rows,) + ticks.shape[2:])

    normed_all = pick_valid(normed_ticks)
    d_output_all = pick_valid(d_output_ticks)
    right_all = pick_valid(right_ticks)

    def one_piece(piece_index):
        first_row = piece_index * rows_here
        part_index = first_row // model_width
        col_offset = first_row % model_width
        left_norm = lax.dynamic_slice_in_dim(normed_all, col_offset, rows_here, 1)
        left_grad = lax.dynamic_slice_in_dim(d_output_all, col_offset, rows_here, 1)
        left_side = jnp.where(part_index == 3, left_grad, left_norm)
        right_side = lax.dynamic_index_in_dim(right_all, part_index, 1, keepdims=False)
        return jnp.einsum("tr,tc->rc", left_side, right_side, preferred_element_type=jnp.float32)

    blocks = lax.map(
        one_piece, jnp.arange(rows_here * lax.axis_size("dp") // rows_here, dtype=jnp.int32)
    )
    gradient = lax.psum_scatter(
        blocks.reshape(rows_here * lax.axis_size("dp"), blocks.shape[2]).astype(jnp.bfloat16),
        "dp",
        scatter_dimension=0,
        tiled=True,
    ).astype(jnp.float32)
    new_master, new_first, new_second = adam_update(
        gradient, master_weights[0], first_moment[0], second_moment[0]
    )
    return (new_master[None], new_first[None], new_second[None])

def block_positions(visible_index, model_width, block_width):
    half_width = model_width // 2
    place = lax.axis_index("mp") * block_width + jnp.arange(block_width, dtype=jnp.int32)
    rate = jnp.exp(
        (place % half_width).astype(jnp.float32) * (-2.0 * math.log(10000.0) / model_width)
    )
    angles = visible_index.astype(jnp.float32)[..., None] * rate
    return jnp.where(place < half_width, jnp.sin(angles), jnp.cos(angles))


def greet(partners):
    barrier = pltpu.get_barrier_semaphore()
    for partner in partners:
        pl.semaphore_signal(
            barrier, inc=1, device_id=partner, device_id_type=pl.DeviceIdType.MESH
        )
    pl.semaphore_wait(barrier, len(partners))


def push(source, target, send_sem, recv_sem, partner):
    return pltpu.make_async_remote_copy(
        src_ref=source,
        dst_ref=target,
        send_sem=send_sem,
        recv_sem=recv_sem,
        device_id=partner,
        device_id_type=pl.DeviceIdType.MESH,
    )


def in_vmem(kernel, operand, out_shape, scratch, collective_id):
    return pl.pallas_call(
        kernel,
        out_shape=out_shape,
        in_specs=[pl.BlockSpec(memory_space=pltpu.VMEM)],
        out_specs=pl.BlockSpec(memory_space=pltpu.VMEM),
        scratch_shapes=scratch,
        compiler_params=pltpu.CompilerParams(
            collective_id=collective_id, has_side_effects=True, vmem_limit_bytes=40 * 2**20
        ),
    )(operand)


def mesh_partners(peers):
    row, col = lax.axis_index("dp"), lax.axis_index("mp")
    along = [{"dp": lax.rem(row + step, peers)} for step in range(1, peers)]
    across = {"mp": lax.rem(col + 2, 4)}
    beside = {"mp": col + 1 - 2 * lax.rem(col, 2)}
    return (along, across, beside)


def gather_kernel(peers, crossing, x_ref, o_ref, *scratch):
    z_send, z_recv, y_send, y_recv, c_send, c_recv = scratch[:6]
    rows, width = x_ref.shape
    row, col = lax.axis_index("dp"), lax.axis_index("mp")
    _, across, beside = mesh_partners(peers)
    lines = ({"dp": lax.rem(row + 1, peers)}, {"dp": lax.rem(row + peers - 1, peers)})
    opposite = {"segment": 1 - lax.axis_index("segment")}
    greet(list(lines) + [across, beside] + ([opposite] if crossing else []))
    over = lax.rem(col + 2, 4)
    held = x_ref
    if crossing:
        held, x_send, x_recv = scratch[6:]
        entering = push(x_ref, held, x_send, x_recv, opposite)
        entering.start()
        entering.wait_recv()

    def source_of(side, away):
        return row - away if side == 0 else row + away

    def there(side, away):
        return row >= away if side == 0 else row + away < peers

    def passes(side):
        return row < peers - 1 if side == 0 else row > 0

    def slot_of(side, away):
        return 0 if away == 0 else side * (peers - 1) + away

    def place(side, away, owner):
        return o_ref.at[
            pl.ds(pl.multiple_of(source_of(side, away) * rows, rows), rows),
            pl.ds(pl.multiple_of(owner * width, width), width),
        ]

    def block(side, away):
        return held if away == 0 else place(side, away, col)

    def onward(side, away):
        at = side * (peers - 1) + away
        target = place(side, away, col)
        return push(block(side, away), target, z_send.at[at], z_recv.at[at], lines[side])

    def sideways(side, away):
        at = slot_of(side, away)
        target = place(side, away, col)
        return push(block(side, away), target, y_send.at[at], y_recv.at[at], across)

    def inward(side, away, both):
        at = slot_of(side, away) + both * (2 * peers - 1)
        target = place(side, away, over if both else col)
        source = target if both else block(side, away)
        return push(source, target, c_send.at[at], c_recv.at[at], beside)

    every = [(0, 0)] + [(side, away) for away in range(1, peers) for side in (0, 1)]

    def where_there(side, away, action):
        if away == 0:
            action(side, away)
        else:
            pl.when(there(side, away))(functools.partial(action, side, away))

    def arrive(side, away):
        if away > 0:
            onward(side, away - 1).wait_recv()
        for way in (0, 1) if away == 0 else (side,):
            if away < peers - 1:
                pl.when(passes(way))(functools.partial(lambda w: onward(w, away).start(), way))
        sideways(side, away).start()
        inward(side, away, 0).start()

    def relay(side, away):
        sideways(side, away).wait_recv()
        inward(side, away, 1).start()

    def finish(side, away):
        inward(side, away, 0).wait_recv()
        inward(side, away, 1).wait_recv()
        for way in (0, 1) if away == 0 else (side,):
            if away < peers - 1:
                pl.when(passes(way))(functools.partial(lambda w: onward(w, away).wait_send(), way))
        sideways(side, away).wait_send()
        inward(side, away, 0).wait_send()
        inward(side, away, 1).wait_send()

    for side, away in every:
        where_there(side, away, arrive)
    own_rows = pl.ds(pl.multiple_of(row * rows, rows), rows)
    o_ref[own_rows, pl.ds(pl.multiple_of(col * width, width), width)] = held[...]
    for side, away in every:
        where_there(side, away, relay)
    for side, away in every:
        where_there(side, away, finish)
    if crossing:
        entering.wait_send()


def gather_tokens(block, crossing=False):
    peers = lax.axis_size("dp")
    shape = (block.shape[0] * peers, block.shape[1] * 4)
    dma = pltpu.SemaphoreType.DMA
    scratch = [dma((2 * peers - 2,))] * 2 + [dma((2 * peers - 1,))] * 2
    scratch += [dma((4 * peers - 2,))] * 2
    if crossing:
        scratch += [pltpu.VMEM(block.shape, block.dtype), dma, dma]
    return in_vmem(
        functools.partial(gather_kernel, peers, crossing),
        block,
        jax.ShapeDtypeStruct(shape, block.dtype),
        scratch,
        5 if crossing else 0,
    )


def exchange_kernel(peers, x_ref, o_ref, send, recv):
    rows = x_ref.shape[0] // peers
    row = lax.axis_index("dp")
    along = mesh_partners(peers)[0]
    greet(along)
    own = pl.ds(pl.multiple_of(row * rows, rows), rows)
    copies = []
    for step in range(1, peers):
        other = lax.rem(row + step, peers)
        theirs = pl.ds(pl.multiple_of(other * rows, rows), rows)
        copies.append(
            push(
                x_ref.at[theirs], o_ref.at[own], send.at[step - 1], recv.at[step - 1], along[step - 1]
            )
        )
        copies[-1].start()
    o_ref[own] = x_ref[own]
    for copy in copies:
        copy.wait()


def exchange_rows(array):
    peers = lax.axis_size("dp")
    return in_vmem(
        functools.partial(exchange_kernel, peers),
        array,
        jax.ShapeDtypeStruct(array.shape, array.dtype),
        [pltpu.SemaphoreType.DMA((peers - 1,))] * 2,
        1 if array.shape[1] % 768 else 2,
    )


def to_last_kernel(peers, x_ref, o_ref, send, recv):
    rows = x_ref.shape[0]
    row = lax.axis_index("dp")
    greet(mesh_partners(peers)[0])

    def copy_from(source):
        return push(
            x_ref,
            o_ref.at[pl.ds(source * rows, rows)],
            send.at[source],
            recv.at[source],
            {"dp": peers - 1},
        )

    for source in range(peers - 1):

        @pl.when(row == source)
        def _():
            copy_from(source).start()
            o_ref[...] = jnp.zeros_like(o_ref)
            copy_from(source).wait_send()

    @pl.when(row == peers - 1)
    def _():
        o_ref[pl.ds((peers - 1) * rows, rows)] = x_ref[...]
        for source in range(peers - 1):
            copy_from(source).wait_recv()


def gather_rows(array):
    peers = lax.axis_size("dp")
    return in_vmem(
        functools.partial(to_last_kernel, peers),
        array,
        jax.ShapeDtypeStruct((array.shape[0] * peers, array.shape[1]), array.dtype),
        [pltpu.SemaphoreType.DMA((peers - 1,))] * 2,
        3,
    )


def from_last_kernel(peers, x_ref, o_ref, send, recv):
    rows = o_ref.shape[0]
    row = lax.axis_index("dp")
    greet(mesh_partners(peers)[0])
    copies = [
        push(
            x_ref.at[pl.ds(target * rows, rows)], o_ref, send.at[target], recv, {"dp": target}
        )
        for target in range(peers - 1)
    ]

    @pl.when(row == peers - 1)
    def _():
        for copy in copies:
            copy.start()
        o_ref[...] = x_ref[pl.ds((peers - 1) * rows, rows)]
        for copy in copies:
            copy.wait_send()

    @pl.when(row < peers - 1)
    def _():
        copies[0].wait_recv()


def scatter_from_last(array):
    peers = lax.axis_size("dp")
    return in_vmem(
        functools.partial(from_last_kernel, peers),
        array,
        jax.ShapeDtypeStruct((array.shape[0] // peers, array.shape[1]), array.dtype),
        [pltpu.SemaphoreType.DMA((peers - 1,)), pltpu.SemaphoreType.DMA],
        6 if array.shape[1] % 768 else 7,
    )


def scatter_kernel(
    peers, x_ref, o_ref, came, passed, landed, c_send, c_recv, y_send, y_recv
):
    width = x_ref.shape[1] // 4
    rows = x_ref.shape[0] // peers
    col = lax.axis_index("mp")
    _, across, beside = mesh_partners(peers)
    greet([across, beside])
    next_to = col + 1 - 2 * lax.rem(col, 2)
    over = lax.rem(col + 2, 4)
    over_next = lax.rem(next_to + 2, 4)

    def piece(step, owner):
        return (
            pl.ds(step * rows, rows),
            pl.ds(pl.multiple_of(owner * width, width), width),
        )

    far, near = [], []
    for step in range(peers):
        for slot, owner, copies in ((0, over_next, far), (1, next_to, near)):
            at = slot * peers + step
            copies.append(
                push(
                    x_ref.at[piece(step, owner)],
                    came.at[slot, pl.ds(step * rows, rows)],
                    c_send.at[at],
                    c_recv.at[at],
                    beside,
                )
            )
            if slot == 0:
                copies[-1].start()
    for copy in near:
        copy.start()
    across_copies = []
    for step in range(peers):
        here = pl.ds(step * rows, rows)
        far[step].wait_recv()
        passed[here] = (
            x_ref[piece(step, over)].astype(jnp.float32) + came[0, here].astype(jnp.float32)
        ).astype(jnp.bfloat16)
        across_copies.append(
            push(passed.at[here], landed.at[here], y_send.at[step], y_recv.at[step], across)
        )
        across_copies[-1].start()
    for step in range(peers):
        here = pl.ds(step * rows, rows)
        near[step].wait_recv()
        across_copies[step].wait_recv()
        o_ref[here] = (
            x_ref[piece(step, col)].astype(jnp.float32)
            + came[1, here].astype(jnp.float32)
            + landed[here].astype(jnp.float32)
        ).astype(jnp.bfloat16)
    for copy in far + near + across_copies:
        copy.wait_send()


def scatter_features(array):
    peers = lax.axis_size("dp")
    shape = (array.shape[0], array.shape[1] // 4)
    dma = pltpu.SemaphoreType.DMA
    return in_vmem(
        functools.partial(scatter_kernel, peers),
        array,
        jax.ShapeDtypeStruct(shape, array.dtype),
        [
            pltpu.VMEM((2,) + shape, jnp.bfloat16),
            pltpu.VMEM(shape, jnp.bfloat16),
            pltpu.VMEM(shape, jnp.bfloat16),
        ]
        + [dma((2 * peers,))] * 2
        + [dma((peers,))] * 2,
        4,
    )


def row_sums(array):
    return jnp.sum(lax.all_gather(array, "mp", axis=0), axis=0)


def sum_rows(array):
    peers = lax.axis_size("dp")
    parts = exchange_rows(array).reshape(peers, array.shape[0] // peers, array.shape[1])
    return jnp.sum(parts[: peers - 1].astype(jnp.float32), axis=0)


def split_heads(array, length):
    return array.reshape(-1, length, array.shape[-1] // HD, HD)


def attend(queries, key_rows, values, length):
    queries, key_rows, values = (split_heads(part, length) for part in (queries, key_rows, values))
    scores = jnp.einsum(
        "vqhe,vkhe->vhqk", queries, key_rows, preferred_element_type=jnp.float32
    ) * (1.0 / math.sqrt(HD))
    probs = softmax_rows(scores)
    attended = jnp.einsum(
        "vhqk,vkhe->vqhe",
        probs.astype(jnp.bfloat16),
        values,
        preferred_element_type=jnp.float32,
    )
    return (probs, attended.astype(jnp.bfloat16).reshape(-1, attended.shape[2] * HD))


def attend_back(queries, key_rows, values, probs, d_attended, length):
    queries, key_rows, values, d_attended = (
        split_heads(part, length) for part in (queries, key_rows, values, d_attended)
    )
    d_probs = jnp.einsum(
        "vqhe,vkhe->vhqk", d_attended, values, preferred_element_type=jnp.float32
    )
    d_scores = (
        probs
        * (d_probs - jnp.sum(d_probs * probs, axis=-1, keepdims=True))
        * (1.0 / math.sqrt(HD))
    ).astype(jnp.bfloat16)
    d_queries = jnp.einsum(
        "vhqk,vkhe->vqhe", d_scores, key_rows, preferred_element_type=jnp.float32
    )
    d_keys = jnp.einsum("vhqk,vqhe->vkhe", d_scores, queries, preferred_element_type=jnp.float32)
    d_values = jnp.einsum(
        "vhqk,vqhe->vkhe",
        probs.astype(jnp.bfloat16),
        d_attended,
        preferred_element_type=jnp.float32,
    )
    return tuple(
        part.astype(jnp.bfloat16).reshape(-1, part.shape[2] * HD)
        for part in (d_queries, d_keys, d_values)
    )


def times_weights(left, weights):
    return jnp.dot(left, weights, preferred_element_type=jnp.float32).astype(jnp.bfloat16)


def times_weights_t(left, weights):
    return lax.dot_general(
        left, weights, (((1,), (1,)), ((), ())), preferred_element_type=jnp.float32
    ).astype(jnp.bfloat16)


def still_shards(
    patch_tokens, visible_index, output_grad, norm_gain, master_weights, first_moment, second_moment
):
    peers = lax.axis_size("dp")
    vol_count, length, block_width = patch_tokens.shape
    model_width = block_width * lax.axis_size("mp")
    rows = vol_count * length
    in_first = lax.axis_index("segment") == 0
    holds_out = lax.axis_index("dp") == peers - 1
    norm_scale = norm_gain[0]
    weights = master_weights[0].astype(jnp.bfloat16)
    own_input = (
        patch_tokens.astype(jnp.float32) + block_positions(visible_index, model_width, block_width)
    ).astype(jnp.bfloat16)
    own_input = own_input.reshape(rows, block_width)
    own_grad = output_grad.reshape(rows, block_width)

    def parts_of(array):
        return [array[i * rows : (i + 1) * rows] for i in range(peers)]

    entered = gather_tokens(jnp.where(in_first, own_input, own_grad))
    normed = norm_forward(entered, norm_scale)[0]
    left_first = jnp.where(holds_out, entered, normed)
    q0, k0, v0, _ = parts_of(exchange_rows(times_weights(left_first, weights)))
    probs0, attended0 = attend(q0, k0, v0, length)
    mixed = scatter_from_last(
        scatter_features(times_weights_t(gather_rows(attended0), weights))
    )
    own_out = (own_input.astype(jnp.float32) + mixed.astype(jnp.float32)).astype(jnp.bfloat16)

    middle = gather_tokens(own_out, True)
    left_second = jnp.where(holds_out, entered, norm_forward(middle, norm_scale)[0])
    q1, k1, v1, da1 = parts_of(exchange_rows(times_weights(left_second, weights)))
    probs1, attended1 = attend(q1, k1, v1, length)
    grads1 = attend_back(q1, k1, v1, probs1, da1, length)
    right_second = exchange_rows(jnp.concatenate(grads1 + (attended1,), axis=0))
    d_normed = sum_rows(scatter_features(times_weights_t(right_second, weights)))

    own_rows = lax.dynamic_slice_in_dim(middle, lax.axis_index("dp") * rows, rows, 0)
    own_cols = lax.axis_index("mp") * block_width
    _, standard, inverse_dev = norm_forward(own_rows, norm_scale)
    standard = lax.dynamic_slice_in_dim(standard, own_cols, block_width, 1)
    scaled = d_normed * lax.dynamic_slice_in_dim(norm_scale, own_cols, block_width, 0)
    sums = row_sums(
        jnp.stack([jnp.sum(scaled, axis=-1), jnp.sum(scaled * standard, axis=-1)])
    ) * (1.0 / model_width)
    inner = scaled - sums[0][:, None] - standard * sums[1][:, None]
    own_d = (own_grad.astype(jnp.float32) + inner * inverse_dev).astype(jnp.bfloat16)

    returned = gather_tokens(own_d, True)
    da0 = scatter_from_last(times_weights(returned, weights))
    grads0 = attend_back(q0, k0, v0, probs0, da0, length)
    right_first = exchange_rows(jnp.concatenate(grads0 + (attended0,), axis=0))

    left_first = jnp.where(holds_out, returned, normed)
    left_side = jnp.where(in_first, left_first, left_second)
    right_side = jnp.where(in_first, right_first, right_second)
    gradient = lax.dot_general(
        left_side, right_side, (((0,), (0,)), ((), ())), preferred_element_type=jnp.float32
    )
    new_master, new_first, new_second = adam_update(
        gradient, master_weights[0], first_moment[0], second_moment[0]
    )
    return (new_master[None], new_first[None], new_second[None])


def section_step(*arrays):
    model_width = arrays[0].shape[2] * lax.axis_size("mp")
    sizes = tuple(lax.axis_size(axis) for axis in ("segment", "dp", "mp"))
    if arrays[4].shape[1] == model_width and sizes == (2, 4, 4):
        return still_shards(*arrays)
    return shards(*arrays)


def solution(mesh):
    placed = (
        P("dp", None, "mp"),
        P("dp", None),
        P("dp", None, "mp"),
        P("segment", None),
        P("segment", "dp", "mp"),
        P("segment", "dp", "mp"),
        P("segment", "dp", "mp"),
    )
    return jax.shard_map(
        section_step,
        mesh=mesh,
        in_specs=placed,
        out_specs=(P("segment", "dp", "mp"), P("segment", "dp", "mp"), P("segment", "dp", "mp")),
        check_vma=False,
    )
```

```python
import functools
import math

import jax
import jax.numpy as jnp
from jax import lax
from jax.experimental import pallas as pl
from jax.experimental.pallas import tpu as pltpu
from jax.sharding import PartitionSpec as P

HD = 128
MB_VOLS = 2
PARTS = 2


beta_one = 0.9
beta_two = 0.95
learn_rate = 0.01
decay_rate = 0.1
adam_eps = 1e-08
norm_eps = 1e-05
step_count = 10


def from_behind(array, axis, by):
    peers = lax.axis_size(axis)
    pairs = [(i, i + by) for i in range(peers) if 0 <= i + by < peers]
    return lax.ppermute(array, axis, pairs)


def position_table(visible_index, model_width):
    half_width = model_width // 2
    angle_rate = jnp.exp(
        jnp.arange(half_width, dtype=jnp.float32) * (-2.0 * math.log(10000.0) / model_width)
    )
    angles = visible_index.astype(jnp.float32)[..., None] * angle_rate
    return jnp.concatenate([jnp.sin(angles), jnp.cos(angles)], axis=-1)


def norm_forward(hidden, norm_scale):
    values = hidden.astype(jnp.float32)
    centred = values - jnp.mean(values, axis=-1, keepdims=True)
    inverse_dev = lax.rsqrt(jnp.mean(centred * centred, axis=-1, keepdims=True) + norm_eps)
    standard = centred * inverse_dev
    return ((standard * norm_scale).astype(jnp.bfloat16), standard, inverse_dev)


def norm_backward(d_normed, d_output, standard, inverse_dev, norm_scale):
    scaled = d_normed * norm_scale
    inner = (
        scaled
        - jnp.mean(scaled, axis=-1, keepdims=True)
        - standard * jnp.mean(scaled * standard, axis=-1, keepdims=True)
    )
    return (d_output.astype(jnp.float32) + inner * inverse_dev).astype(jnp.bfloat16)


def softmax_rows(scores):
    lifted = jnp.exp(scores - jnp.max(scores, axis=-1, keepdims=True))
    return lifted / jnp.sum(lifted, axis=-1, keepdims=True)


def rounded(values):
    return lax.optimization_barrier(values.astype(jnp.bfloat16)).astype(jnp.float32)


def adam_update(gradient, master, first_moment, second_moment):
    new_first = beta_one * first_moment + (1.0 - beta_one) * gradient
    new_second = beta_two * second_moment + (1.0 - beta_two) * gradient * gradient
    direction = (
        new_first
        / (1.0 - beta_one**step_count)
        / (jnp.sqrt(new_second / (1.0 - beta_two**step_count)) + adam_eps)
    )
    new_master = master - learn_rate * (direction + decay_rate * master)
    return (new_master, new_first, new_second)


def layer_local(layer_in, norm_scale, weights):
    row_count, model_width = layer_in.shape
    col_count = weights.shape[1]
    head_count = col_count // HD
    length = row_count // MB_VOLS
    normed, standard, inverse_dev = norm_forward(layer_in, norm_scale)
    triple = weights[: 3 * model_width].reshape(3, model_width, col_count)
    project = jnp.einsum("nd,sdc->nsc", normed, triple, preferred_element_type=jnp.float32).astype(
        jnp.bfloat16
    )
    shaped = project.reshape(MB_VOLS, length, 3, head_count, HD)
    scores = jnp.einsum(
        "vqhe,vkhe->vhqk", shaped[:, :, 0], shaped[:, :, 1], preferred_element_type=jnp.float32
    ) * (1.0 / math.sqrt(HD))
    softmaxed = softmax_rows(scores)
    probs_half = softmaxed.astype(jnp.bfloat16)
    attended = jnp.einsum(
        "vhqk,vkhe->vqhe", probs_half, shaped[:, :, 2], preferred_element_type=jnp.float32
    )
    attended = attended.astype(jnp.bfloat16).reshape(row_count, col_count)
    return (normed, standard, inverse_dev, project, softmaxed, probs_half, attended)


def head_terms(attended, weights, model_width):
    return rounded(
        jnp.einsum(
            "nc,dc->nd", attended, weights[3 * model_width :], preferred_element_type=jnp.float32
        )
    )


def attention_back(d_output, saved_vals, weights):
    project, softmaxed, probs_half = (saved_vals[3], saved_vals[4], saved_vals[5])
    row_count, model_width = d_output.shape
    col_count = weights.shape[1]
    head_count = col_count // HD
    length = row_count // MB_VOLS
    shaped = project.reshape(MB_VOLS, length, 3, head_count, HD)
    d_attended = jnp.einsum(
        "nd,dc->nc", d_output, weights[3 * model_width :], preferred_element_type=jnp.float32
    )
    d_attended = d_attended.astype(jnp.bfloat16).reshape(MB_VOLS, length, head_count, HD)
    d_probs = jnp.einsum(
        "vqhe,vkhe->vhqk", d_attended, shaped[:, :, 2], preferred_element_type=jnp.float32
    )
    d_scores = (
        softmaxed
        * (d_probs - jnp.sum(d_probs * softmaxed, axis=-1, keepdims=True))
        * (1.0 / math.sqrt(HD))
    ).astype(jnp.bfloat16)
    d_queries = jnp.einsum(
        "vhqk,vkhe->vqhe", d_scores, shaped[:, :, 1], preferred_element_type=jnp.float32
    ).astype(jnp.bfloat16)
    d_keys = jnp.einsum(
        "vhqk,vqhe->vkhe", d_scores, shaped[:, :, 0], preferred_element_type=jnp.float32
    ).astype(jnp.bfloat16)
    d_values = jnp.einsum(
        "vhqk,vqhe->vkhe", probs_half, d_attended, preferred_element_type=jnp.float32
    ).astype(jnp.bfloat16)
    return jnp.stack([d_queries, d_keys, d_values], axis=2).reshape(row_count, 3, col_count)


def feature_terms(d_project, weights, model_width):
    col_count = weights.shape[1]
    triple = weights[: 3 * model_width].reshape(3, model_width, col_count)
    return rounded(jnp.einsum("nsc,sdc->nd", d_project, triple, preferred_element_type=jnp.float32))


def shards(
    patch_tokens, visible_index, output_grad, norm_gain, master_weights, first_moment, second_moment
):
    model_width = patch_tokens.shape[2] * lax.axis_size("mp")
    rows_here = master_weights.shape[1]
    is_first = lax.axis_index("segment") == 0
    norm_scale = norm_gain[0]
    weights = lax.all_gather(master_weights[0].astype(jnp.bfloat16), "dp", axis=0, tiled=True)
    tokens_full, grads_full = (
        lax.all_gather(patch_tokens, "mp", axis=2, tiled=True),
        lax.all_gather(output_grad, "mp", axis=2, tiled=True),
    )
    vol_count, length = visible_index.shape
    micro_count = vol_count // MB_VOLS
    mb_rows = MB_VOLS * length
    first_inputs = (
        tokens_full.astype(jnp.float32) + position_table(visible_index, model_width)
    ).astype(jnp.bfloat16)
    first_inputs = first_inputs.reshape(micro_count, mb_rows, model_width)
    out_grads = grads_full.reshape(micro_count, mb_rows, model_width)
    zeros_full = jnp.zeros((mb_rows, model_width), jnp.bfloat16)
    saved_ticks = []
    received = zeros_full
    for step_index in range(micro_count + 1):
        arriving = received
        own_input = first_inputs[step_index] if step_index < micro_count else zeros_full
        layer_in = jnp.where(is_first, own_input, arriving)
        saved_vals = layer_local(layer_in, norm_scale, weights)
        saved_ticks.append(saved_vals)
        if step_index < micro_count:
            head_part = head_terms(saved_vals[6], weights, model_width)
            mixed = lax.psum(head_part.astype(jnp.bfloat16), "mp").astype(jnp.float32)
            layer_out = (layer_in.astype(jnp.float32) + mixed).astype(jnp.bfloat16)
            received = from_behind(layer_out, "segment", 1)
    back_ticks = []
    for step_index in range(micro_count + 1):
        arriving = received if step_index > 0 else zeros_full
        own_grad = (
            out_grads[micro_count - 1 - step_index] if step_index < micro_count else zeros_full
        )
        d_output = jnp.where(is_first, arriving, own_grad)
        saved_vals = saved_ticks[micro_count - step_index]
        d_project = attention_back(d_output, saved_vals, weights)
        back_ticks.append((d_output, d_project))
        if step_index < micro_count:
            d_terms = feature_terms(d_project, weights, model_width)
            standard, inverse_dev = (saved_vals[1], saved_vals[2])
            summed = lax.psum(d_terms.astype(jnp.bfloat16), "mp").astype(jnp.float32)
            d_input = norm_backward(summed, d_output, standard, inverse_dev, norm_scale)
            received = from_behind(d_input, "segment", -1)
    all_steps = range(micro_count + 1)
    normed_ticks = jnp.stack([saved_ticks[micro_count - step_index][0] for step_index in all_steps])
    attended_ticks = jnp.stack(
        [saved_ticks[micro_count - step_index][6] for step_index in all_steps]
    )
    d_output_ticks = jnp.stack([back_ticks[step_index][0] for step_index in all_steps])
    d_project_ticks = jnp.stack([back_ticks[step_index][1] for step_index in all_steps])
    right_ticks = jnp.concatenate([d_project_ticks, attended_ticks[:, :, None]], axis=2)

    def pick_valid(ticks):
        chosen = jnp.where(is_first, ticks[1:], ticks[:-1])
        return chosen.reshape((micro_count * mb_rows,) + ticks.shape[2:])

    normed_all = pick_valid(normed_ticks)
    d_output_all = pick_valid(d_output_ticks)
    right_all = pick_valid(right_ticks)

    def one_piece(piece_index):
        first_row = piece_index * rows_here
        part_index = first_row // model_width
        col_offset = first_row % model_width
        left_norm = lax.dynamic_slice_in_dim(normed_all, col_offset, rows_here, 1)
        left_grad = lax.dynamic_slice_in_dim(d_output_all, col_offset, rows_here, 1)
        left_side = jnp.where(part_index == 3, left_grad, left_norm)
        right_side = lax.dynamic_index_in_dim(right_all, part_index, 1, keepdims=False)
        return jnp.einsum("tr,tc->rc", left_side, right_side, preferred_element_type=jnp.float32)

    blocks = lax.map(
        one_piece, jnp.arange(rows_here * lax.axis_size("dp") // rows_here, dtype=jnp.int32)
    )
    gradient = lax.psum_scatter(
        blocks.reshape(rows_here * lax.axis_size("dp"), blocks.shape[2]).astype(jnp.bfloat16),
        "dp",
        scatter_dimension=0,
        tiled=True,
    ).astype(jnp.float32)
    new_master, new_first, new_second = adam_update(
        gradient, master_weights[0], first_moment[0], second_moment[0]
    )
    return (new_master[None], new_first[None], new_second[None])

def block_positions(visible_index, model_width, block_width):
    half_width = model_width // 2
    place = lax.axis_index("mp") * block_width + jnp.arange(block_width, dtype=jnp.int32)
    rate = jnp.exp(
        (place % half_width).astype(jnp.float32) * (-2.0 * math.log(10000.0) / model_width)
    )
    angles = visible_index.astype(jnp.float32)[..., None] * rate
    return jnp.where(place < half_width, jnp.sin(angles), jnp.cos(angles))


def greet(partners):
    barrier = pltpu.get_barrier_semaphore()
    for partner in partners:
        pl.semaphore_signal(
            barrier, inc=1, device_id=partner, device_id_type=pl.DeviceIdType.MESH
        )
    pl.semaphore_wait(barrier, len(partners))


def push(source, target, send_sem, recv_sem, partner):
    return pltpu.make_async_remote_copy(
        src_ref=source,
        dst_ref=target,
        send_sem=send_sem,
        recv_sem=recv_sem,
        device_id=partner,
        device_id_type=pl.DeviceIdType.MESH,
    )


def in_vmem(kernel, operand, out_shape, scratch, collective_id):
    return pl.pallas_call(
        kernel,
        out_shape=out_shape,
        in_specs=[pl.BlockSpec(memory_space=pltpu.VMEM)],
        out_specs=pl.BlockSpec(memory_space=pltpu.VMEM),
        scratch_shapes=scratch,
        compiler_params=pltpu.CompilerParams(
            collective_id=collective_id, has_side_effects=True, vmem_limit_bytes=40 * 2**20
        ),
    )(operand)


def mesh_partners(peers):
    row, col = lax.axis_index("dp"), lax.axis_index("mp")
    along = [{"dp": lax.rem(row + step, peers)} for step in range(1, peers)]
    across = {"mp": lax.rem(col + 2, 4)}
    beside = {"mp": col + 1 - 2 * lax.rem(col, 2)}
    return (along, across, beside)


def gather_kernel(peers, crossing, x_ref, o_ref, *scratch):
    z_send, z_recv, y_send, y_recv, c_send, c_recv = scratch[:6]
    rows, width = x_ref.shape[0] // PARTS, x_ref.shape[1]
    row, col = lax.axis_index("dp"), lax.axis_index("mp")
    _, across, beside = mesh_partners(peers)
    lines = ({"dp": lax.rem(row + 1, peers)}, {"dp": lax.rem(row + peers - 1, peers)})
    opposite = {"segment": 1 - lax.axis_index("segment")}
    greet(list(lines) + [across, beside] + ([opposite] if crossing else []))
    over = lax.rem(col + 2, 4)
    held = x_ref
    if crossing:
        held, x_send, x_recv = scratch[6:]
        pieces = [pl.ds(part * rows, rows) for part in range(PARTS)]
        entering = [
            push(x_ref.at[piece], held.at[piece], x_send.at[part], x_recv.at[part], opposite)
            for part, piece in enumerate(pieces)
        ]
        for copy in entering:
            copy.start()

    def source_of(side, away):
        return row - away if side == 0 else row + away

    def there(side, away):
        return row >= away if side == 0 else row + away < peers

    def passes(side):
        return row < peers - 1 if side == 0 else row > 0

    def slot_of(side, away):
        return 0 if away == 0 else side * (peers - 1) + away

    def place(part, side, away, owner):
        return o_ref.at[
            pl.ds(
                pl.multiple_of((source_of(side, away) * PARTS + part) * rows, rows), rows
            ),
            pl.ds(pl.multiple_of(owner * width, width), width),
        ]

    def block(part, side, away):
        return held.at[pl.ds(part * rows, rows)] if away == 0 else place(part, side, away, col)

    def onward(part, side, away):
        at = (part * 2 + side) * (peers - 1) + away
        target = place(part, side, away, col)
        return push(block(part, side, away), target, z_send.at[at], z_recv.at[at], lines[side])

    def sideways(part, side, away):
        at = slot_of(side, away) + part * (2 * peers - 1)
        target = place(part, side, away, col)
        return push(block(part, side, away), target, y_send.at[at], y_recv.at[at], across)

    def inward(part, side, away, both):
        at = slot_of(side, away) + (part * 2 + both) * (2 * peers - 1)
        target = place(part, side, away, over if both else col)
        source = target if both else block(part, side, away)
        return push(source, target, c_send.at[at], c_recv.at[at], beside)

    spots = [(0, 0)] + [(side, away) for away in range(1, peers) for side in (0, 1)]
    every = [(part, side, away) for side, away in spots for part in range(PARTS)]

    def where_there(part, side, away, action):
        if away == 0:
            action(part, side, away)
        else:
            pl.when(there(side, away))(functools.partial(action, part, side, away))

    def arrive(part, side, away):
        if away > 0:
            onward(part, side, away - 1).wait_recv()
        elif crossing:
            entering[part].wait_recv()
        for way in (0, 1) if away == 0 else (side,):
            if away < peers - 1:
                pl.when(passes(way))(functools.partial(lambda w: onward(part, w, away).start(), way))
        sideways(part, side, away).start()
        inward(part, side, away, 0).start()

    def relay(part, side, away):
        sideways(part, side, away).wait_recv()
        inward(part, side, away, 1).start()

    def finish(part, side, away):
        inward(part, side, away, 0).wait_recv()
        inward(part, side, away, 1).wait_recv()
        for way in (0, 1) if away == 0 else (side,):
            if away < peers - 1:
                pl.when(passes(way))(functools.partial(lambda w: onward(part, w, away).wait_send(), way))
        sideways(part, side, away).wait_send()
        inward(part, side, away, 0).wait_send()
        inward(part, side, away, 1).wait_send()

    for part, side, away in every:
        where_there(part, side, away, arrive)
    own_rows = pl.ds(pl.multiple_of(row * PARTS * rows, rows), PARTS * rows)
    o_ref[own_rows, pl.ds(pl.multiple_of(col * width, width), width)] = held[...]
    for part, side, away in every:
        where_there(part, side, away, relay)
    for part, side, away in every:
        where_there(part, side, away, finish)
    if crossing:
        for copy in entering:
            copy.wait_send()


def gather_tokens(block, crossing=False):
    peers = lax.axis_size("dp")
    shape = (block.shape[0] * peers, block.shape[1] * 4)
    dma = pltpu.SemaphoreType.DMA
    scratch = [dma((PARTS * (2 * peers - 2),))] * 2 + [dma((PARTS * (2 * peers - 1),))] * 2
    scratch += [dma((PARTS * (4 * peers - 2),))] * 2
    if crossing:
        scratch += [pltpu.VMEM(block.shape, block.dtype), dma((PARTS,)), dma((PARTS,))]
    return in_vmem(
        functools.partial(gather_kernel, peers, crossing),
        block,
        jax.ShapeDtypeStruct(shape, block.dtype),
        scratch,
        5 if crossing else 0,
    )


def exchange_kernel(peers, x_ref, o_ref, send, recv):
    rows = x_ref.shape[0] // peers
    row = lax.axis_index("dp")
    along = mesh_partners(peers)[0]
    greet(along)
    own = pl.ds(pl.multiple_of(row * rows, rows), rows)
    copies = []
    for step in range(1, peers):
        other = lax.rem(row + step, peers)
        theirs = pl.ds(pl.multiple_of(other * rows, rows), rows)
        copies.append(
            push(
                x_ref.at[theirs], o_ref.at[own], send.at[step - 1], recv.at[step - 1], along[step - 1]
            )
        )
        copies[-1].start()
    o_ref[own] = x_ref[own]
    for copy in copies:
        copy.wait()


def exchange_rows(array):
    peers = lax.axis_size("dp")
    return in_vmem(
        functools.partial(exchange_kernel, peers),
        array,
        jax.ShapeDtypeStruct(array.shape, array.dtype),
        [pltpu.SemaphoreType.DMA((peers - 1,))] * 2,
        1 if array.shape[1] % 768 else 2,
    )


def to_last_kernel(peers, x_ref, o_ref, send, recv):
    rows = x_ref.shape[0]
    row = lax.axis_index("dp")
    greet(mesh_partners(peers)[0])

    def copy_from(source):
        return push(
            x_ref,
            o_ref.at[pl.ds(source * rows, rows)],
            send.at[source],
            recv.at[source],
            {"dp": peers - 1},
        )

    for source in range(peers - 1):

        @pl.when(row == source)
        def _():
            copy_from(source).start()
            o_ref[...] = jnp.zeros_like(o_ref)
            copy_from(source).wait_send()

    @pl.when(row == peers - 1)
    def _():
        o_ref[pl.ds((peers - 1) * rows, rows)] = x_ref[...]
        for source in range(peers - 1):
            copy_from(source).wait_recv()


def gather_rows(array):
    peers = lax.axis_size("dp")
    return in_vmem(
        functools.partial(to_last_kernel, peers),
        array,
        jax.ShapeDtypeStruct((array.shape[0] * peers, array.shape[1]), array.dtype),
        [pltpu.SemaphoreType.DMA((peers - 1,))] * 2,
        3,
    )


def from_last_kernel(peers, x_ref, o_ref, send, recv):
    rows = o_ref.shape[0]
    row = lax.axis_index("dp")
    greet(mesh_partners(peers)[0])
    copies = [
        push(
            x_ref.at[pl.ds(target * rows, rows)], o_ref, send.at[target], recv, {"dp": target}
        )
        for target in range(peers - 1)
    ]

    @pl.when(row == peers - 1)
    def _():
        for copy in copies:
            copy.start()
        o_ref[...] = x_ref[pl.ds((peers - 1) * rows, rows)]
        for copy in copies:
            copy.wait_send()

    @pl.when(row < peers - 1)
    def _():
        copies[0].wait_recv()


def scatter_from_last(array):
    peers = lax.axis_size("dp")
    return in_vmem(
        functools.partial(from_last_kernel, peers),
        array,
        jax.ShapeDtypeStruct((array.shape[0] // peers, array.shape[1]), array.dtype),
        [pltpu.SemaphoreType.DMA((peers - 1,)), pltpu.SemaphoreType.DMA],
        6 if array.shape[1] % 768 else 7,
    )


def scatter_kernel(
    peers, x_ref, o_ref, came, passed, landed, c_send, c_recv, y_send, y_recv
):
    width = x_ref.shape[1] // 4
    rows = x_ref.shape[0] // peers
    col = lax.axis_index("mp")
    _, across, beside = mesh_partners(peers)
    greet([across, beside])
    next_to = col + 1 - 2 * lax.rem(col, 2)
    over = lax.rem(col + 2, 4)
    over_next = lax.rem(next_to + 2, 4)

    def piece(step, owner):
        return (
            pl.ds(step * rows, rows),
            pl.ds(pl.multiple_of(owner * width, width), width),
        )

    far, near = [], []
    for step in range(peers):
        for slot, owner, copies in ((0, over_next, far), (1, next_to, near)):
            at = slot * peers + step
            copies.append(
                push(
                    x_ref.at[piece(step, owner)],
                    came.at[slot, pl.ds(step * rows, rows)],
                    c_send.at[at],
                    c_recv.at[at],
                    beside,
                )
            )
            if slot == 0:
                copies[-1].start()
    for copy in near:
        copy.start()
    across_copies = []
    for step in range(peers):
        here = pl.ds(step * rows, rows)
        far[step].wait_recv()
        passed[here] = (
            x_ref[piece(step, over)].astype(jnp.float32) + came[0, here].astype(jnp.float32)
        ).astype(jnp.bfloat16)
        across_copies.append(
            push(passed.at[here], landed.at[here], y_send.at[step], y_recv.at[step], across)
        )
        across_copies[-1].start()
    for step in range(peers):
        here = pl.ds(step * rows, rows)
        near[step].wait_recv()
        across_copies[step].wait_recv()
        o_ref[here] = (
            x_ref[piece(step, col)].astype(jnp.float32)
            + came[1, here].astype(jnp.float32)
            + landed[here].astype(jnp.float32)
        ).astype(jnp.bfloat16)
    for copy in far + near + across_copies:
        copy.wait_send()


def scatter_features(array):
    peers = lax.axis_size("dp")
    shape = (array.shape[0], array.shape[1] // 4)
    dma = pltpu.SemaphoreType.DMA
    return in_vmem(
        functools.partial(scatter_kernel, peers),
        array,
        jax.ShapeDtypeStruct(shape, array.dtype),
        [
            pltpu.VMEM((2,) + shape, jnp.bfloat16),
            pltpu.VMEM(shape, jnp.bfloat16),
            pltpu.VMEM(shape, jnp.bfloat16),
        ]
        + [dma((2 * peers,))] * 2
        + [dma((peers,))] * 2,
        4,
    )


def row_sums(array):
    return jnp.sum(lax.all_gather(array, "mp", axis=0), axis=0)


def sum_rows(array):
    peers = lax.axis_size("dp")
    parts = exchange_rows(array).reshape(peers, array.shape[0] // peers, array.shape[1])
    return jnp.sum(parts[: peers - 1].astype(jnp.float32), axis=0)


def split_heads(array, length):
    return array.reshape(-1, length, array.shape[-1] // HD, HD)


def attend(queries, key_rows, values, length):
    queries, key_rows, values = (split_heads(part, length) for part in (queries, key_rows, values))
    scores = jnp.einsum(
        "vqhe,vkhe->vhqk", queries, key_rows, preferred_element_type=jnp.float32
    ) * (1.0 / math.sqrt(HD))
    probs = softmax_rows(scores)
    attended = jnp.einsum(
        "vhqk,vkhe->vqhe",
        probs.astype(jnp.bfloat16),
        values,
        preferred_element_type=jnp.float32,
    )
    return (probs, attended.astype(jnp.bfloat16).reshape(-1, attended.shape[2] * HD))


def attend_back(queries, key_rows, values, probs, d_attended, length):
    queries, key_rows, values, d_attended = (
        split_heads(part, length) for part in (queries, key_rows, values, d_attended)
    )
    d_probs = jnp.einsum(
        "vqhe,vkhe->vhqk", d_attended, values, preferred_element_type=jnp.float32
    )
    d_scores = (
        probs
        * (d_probs - jnp.sum(d_probs * probs, axis=-1, keepdims=True))
        * (1.0 / math.sqrt(HD))
    ).astype(jnp.bfloat16)
    d_queries = jnp.einsum(
        "vhqk,vkhe->vqhe", d_scores, key_rows, preferred_element_type=jnp.float32
    )
    d_keys = jnp.einsum("vhqk,vqhe->vkhe", d_scores, queries, preferred_element_type=jnp.float32)
    d_values = jnp.einsum(
        "vhqk,vqhe->vkhe",
        probs.astype(jnp.bfloat16),
        d_attended,
        preferred_element_type=jnp.float32,
    )
    return tuple(
        part.astype(jnp.bfloat16).reshape(-1, part.shape[2] * HD)
        for part in (d_queries, d_keys, d_values)
    )


def times_weights(left, weights):
    return jnp.dot(left, weights, preferred_element_type=jnp.float32).astype(jnp.bfloat16)


def times_weights_t(left, weights):
    return lax.dot_general(
        left, weights, (((1,), (1,)), ((), ())), preferred_element_type=jnp.float32
    ).astype(jnp.bfloat16)


def still_shards(
    patch_tokens, visible_index, output_grad, norm_gain, master_weights, first_moment, second_moment
):
    peers = lax.axis_size("dp")
    vol_count, length, block_width = patch_tokens.shape
    model_width = block_width * lax.axis_size("mp")
    rows = vol_count * length
    in_first = lax.axis_index("segment") == 0
    holds_out = lax.axis_index("dp") == peers - 1
    norm_scale = norm_gain[0]
    weights = master_weights[0].astype(jnp.bfloat16)
    own_input = (
        patch_tokens.astype(jnp.float32) + block_positions(visible_index, model_width, block_width)
    ).astype(jnp.bfloat16)
    own_input = own_input.reshape(rows, block_width)
    own_grad = output_grad.reshape(rows, block_width)

    def parts_of(array):
        return [array[i * rows : (i + 1) * rows] for i in range(peers)]

    entered = gather_tokens(jnp.where(in_first, own_input, own_grad))
    normed = norm_forward(entered, norm_scale)[0]
    left_first = jnp.where(holds_out, entered, normed)
    q0, k0, v0, _ = parts_of(exchange_rows(times_weights(left_first, weights)))
    probs0, attended0 = attend(q0, k0, v0, length)
    mixed = scatter_from_last(
        scatter_features(times_weights_t(gather_rows(attended0), weights))
    )
    own_out = (own_input.astype(jnp.float32) + mixed.astype(jnp.float32)).astype(jnp.bfloat16)

    middle = gather_tokens(own_out, True)
    left_second = jnp.where(holds_out, entered, norm_forward(middle, norm_scale)[0])
    q1, k1, v1, da1 = parts_of(exchange_rows(times_weights(left_second, weights)))
    probs1, attended1 = attend(q1, k1, v1, length)
    grads1 = attend_back(q1, k1, v1, probs1, da1, length)
    right_second = exchange_rows(jnp.concatenate(grads1 + (attended1,), axis=0))
    d_normed = sum_rows(scatter_features(times_weights_t(right_second, weights)))

    own_rows = lax.dynamic_slice_in_dim(middle, lax.axis_index("dp") * rows, rows, 0)
    own_cols = lax.axis_index("mp") * block_width
    _, standard, inverse_dev = norm_forward(own_rows, norm_scale)
    standard = lax.dynamic_slice_in_dim(standard, own_cols, block_width, 1)
    scaled = d_normed * lax.dynamic_slice_in_dim(norm_scale, own_cols, block_width, 0)
    sums = row_sums(
        jnp.stack([jnp.sum(scaled, axis=-1), jnp.sum(scaled * standard, axis=-1)])
    ) * (1.0 / model_width)
    inner = scaled - sums[0][:, None] - standard * sums[1][:, None]
    own_d = (own_grad.astype(jnp.float32) + inner * inverse_dev).astype(jnp.bfloat16)

    returned = gather_tokens(own_d, True)
    da0 = scatter_from_last(times_weights(returned, weights))
    grads0 = attend_back(q0, k0, v0, probs0, da0, length)
    right_first = exchange_rows(jnp.concatenate(grads0 + (attended0,), axis=0))

    left_first = jnp.where(holds_out, returned, normed)
    left_side = jnp.where(in_first, left_first, left_second)
    right_side = jnp.where(in_first, right_first, right_second)
    gradient = lax.dot_general(
        left_side, right_side, (((0,), (0,)), ((), ())), preferred_element_type=jnp.float32
    )
    new_master, new_first, new_second = adam_update(
        gradient, master_weights[0], first_moment[0], second_moment[0]
    )
    return (new_master[None], new_first[None], new_second[None])


def section_step(*arrays):
    model_width = arrays[0].shape[2] * lax.axis_size("mp")
    sizes = tuple(lax.axis_size(axis) for axis in ("segment", "dp", "mp"))
    if arrays[4].shape[1] == model_width and sizes == (2, 4, 4):
        return still_shards(*arrays)
    return shards(*arrays)


def solution(mesh):
    placed = (
        P("dp", None, "mp"),
        P("dp", None),
        P("dp", None, "mp"),
        P("segment", None),
        P("segment", "dp", "mp"),
        P("segment", "dp", "mp"),
        P("segment", "dp", "mp"),
    )
    return jax.shard_map(
        section_step,
        mesh=mesh,
        in_specs=placed,
        out_specs=(P("segment", "dp", "mp"), P("segment", "dp", "mp"), P("segment", "dp", "mp")),
        check_vma=False,
    )
```
